32 devices in a mesh: band: 4 (over y, x), dom: 8 (over z, core).
Axes of the slice: x: 2, y: 2, z: 4, core: 2. Of those that a mesh axis runs over, the one named last changes fastest.
Arguments:
- orbitals: bfloat16 [8, 1408, 800], P('dom', 'band'), may hold values from -6 to 6
- rotation: bfloat16 [800, 800], replicated, may hold values from -0.21875 to 0.21875
- cell_stiffness: bfloat16 [729, 729], replicated, as said below
- cell_scale: float32 [8, 2], P('dom'), may hold values from 0.25 to 1
- potential: float32 [8, 1408], P('dom'), may hold values from 0.25 to 2
- cell_nodes: int32 [8, 2, 729], P('dom'), may hold values from 0 to 2055, as said below
- send_rows: int32 [8, 4, 162], P('dom'), may hold values from 0 to 1408, as said below
- domain_rows: int32 [8], P('dom'), may hold values from 729 to 1377, as said below
Outputs:
- filtered: bfloat16 [8, 1408, 800], P('dom', None, 'band')
The draws below stay inside these ranges and needn't reach their ends.
Inputs may be any that keep to these rules, and one draw needn't show every extreme that they name: Domain d holds n_d cells with domain_rows[d] = 81 * (8 * n_d + 1) and n_d from 1 to 2; some domain holds 2 cells. `cell_nodes`: an entry below 1408 is an owned row of the domain, below its domain_rows for cells below its cell count; an entry 1408 + g * 162 + s is ghost slot s shared with domain d + o_g, o = (1, 8, -8, -1), and appears only where that domain exists. Consecutive cells of a domain share a layer of nodes. send_rows[e, g, s] is the owned row of domain e, below domain_rows[e], whose value ghost slot s of group g of domain e - o_g holds, o = (1, 8, -8, -1); 1408 marks a slot that no cell uses. Some domain fills all 162 slots of one group. `cell_stiffness`: A symmetric matrix.
All inputs are finite; a program needn't handle non-finite values.
Results may differ from the reference program's by a relative error of at most 0.0062.
Values may be sent and summed in bfloat16 or wider, within the bound.
No kernel may reach another device: no remote copies, remote signals or barrier semaphores. Data moves between devices by JAX's collectives and lax.ppermute only.
A program may use at most 64 MiB of HBM per device.

```python
import math
import jax
import jax.numpy as jnp
from jax import lax

GROUP_WIDTH = 200
DEGREE = 8
CELL_CAP = 2
FILTER_STEPS = 3
FACES_MAX = 2
GROUPS = 4
BANDS = 800
DOMAINS = 8
CELL_NODES = 729
FACE_NODES = 81
GHOST_SLOTS = 162
OWN_CAP = 1408
N_BAND = 4


OFFSETS = (1, 8, -8, -1)


def mesh_layout(key):
    base_key = jax.random.fold_in(key, 7103)
    key_cells, key_pick, key_full, key_owner = jax.random.split(base_key, 4)
    domain_index = jnp.arange(DOMAINS, dtype=jnp.int32)
    cell_index = jnp.arange(CELL_CAP, dtype=jnp.int32)
    counts = jax.random.randint(key_cells, (DOMAINS,), CELL_CAP // 2, CELL_CAP + 1, dtype=jnp.int32)
    full_domain = jax.random.randint(key_full, (), 1, DOMAINS, dtype=jnp.int32)
    counts = jnp.where(domain_index == full_domain, CELL_CAP, counts)
    group_pick = jax.random.randint(key_pick, (DOMAINS, CELL_CAP), 0, GROUPS, dtype=jnp.int32)
    forced = (domain_index[:, None] == full_domain) & (cell_index[None, :] < FACES_MAX)
    group_pick = jnp.where(forced, GROUPS - 1, group_pick)
    offsets = jnp.array(OFFSETS, dtype=jnp.int32)
    group_ids = jnp.arange(GROUPS, dtype=jnp.int32)
    group_fill = jnp.zeros((DOMAINS, GROUPS), jnp.int32)
    face_group = []
    face_place = []
    for cell_pos in range(CELL_CAP):
        chosen = group_pick[:, cell_pos]
        partner = domain_index + offsets[chosen]
        hit_group = group_ids[None, :] == chosen[:, None]
        taken_faces = jnp.sum(jnp.where(hit_group, group_fill, 0), axis=1)
        usable = (cell_pos < counts) & (partner >= 0) & (partner < DOMAINS) & (taken_faces < FACES_MAX)
        face_group.append(jnp.where(usable, chosen, -1))
        face_place.append(taken_faces)
        group_fill = group_fill + (hit_group & usable[:, None]).astype(jnp.int32)
    face_group = jnp.stack(face_group, axis=1)
    face_place = jnp.stack(face_place, axis=1)
    partner_domain = jnp.clip(domain_index[:, None] + offsets[jnp.maximum(face_group, 0)], 0, DOMAINS - 1)
    partner_cells = counts[partner_domain]
    owner_cell = jax.random.randint(key_owner, (DOMAINS, CELL_CAP), 0, partner_cells, dtype=jnp.int32)
    edge_nodes = DEGREE + 1
    node_index = jnp.arange(CELL_NODES, dtype=jnp.int32)
    first_coord = node_index // FACE_NODES
    second_coord = node_index // edge_nodes % edge_nodes
    third_coord = node_index % edge_nodes
    owned_row = (DEGREE * cell_index[None, :, None] + third_coord[None, None, :]) * FACE_NODES + first_coord[None, None, :] * edge_nodes + second_coord[None, None, :]
    ghost_row = OWN_CAP + face_group[:, :, None] * GHOST_SLOTS + face_place[:, :, None] * FACE_NODES + second_coord[None, None, :] * edge_nodes + third_coord[None, None, :]
    is_ghost = (first_coord[None, None, :] == 0) & (face_group[:, :, None] >= 0)
    cell_nodes = jnp.where(is_ghost, ghost_row, owned_row).astype(jnp.int32)
    face_node = jnp.arange(FACE_NODES, dtype=jnp.int32)
    face_second = face_node // edge_nodes
    face_third = face_node % edge_nodes
    owner_rows = (DEGREE * owner_cell[:, :, None] + face_third[None, None, :]) * FACE_NODES + DEGREE * edge_nodes + face_second[None, None, :]
    target_group = jnp.where(face_group >= 0, face_group, GROUPS)
    slot_index = face_place[:, :, None] * FACE_NODES + face_node[None, None, :]
    full_shape = slot_index.shape
    ghost_view = jnp.full((DOMAINS, GROUPS, GHOST_SLOTS), OWN_CAP, jnp.int32)
    ghost_view = ghost_view.at[jnp.broadcast_to(domain_index[:, None, None], full_shape), jnp.broadcast_to(target_group[:, :, None], full_shape), slot_index].set(owner_rows.astype(jnp.int32), mode='drop')
    columns = []
    for group_pos, offset in enumerate(OFFSETS):
        source = domain_index - offset
        in_range = (source >= 0) & (source < DOMAINS)
        picked = ghost_view[jnp.clip(source, 0, DOMAINS - 1), group_pos]
        columns.append(jnp.where(in_range[:, None], picked, OWN_CAP))
    send_rows = jnp.stack(columns, axis=1).astype(jnp.int32)
    domain_rows = (FACE_NODES * (DEGREE * counts + 1)).astype(jnp.int32)
    return (cell_nodes, send_rows, domain_rows)


def draw_cell_nodes(key, part):
    return mesh_layout(key)[0]


def draw_send_rows(key, part):
    return mesh_layout(key)[1]


def draw_domain_rows(key, part):
    return mesh_layout(key)[2]


def draw_cell_stiffness(key, part):
    key_noise, key_diag = jax.random.split(jax.random.fold_in(key, 9001))
    noise = jax.random.normal(key_noise, (CELL_NODES, CELL_NODES), jnp.float32) / jnp.sqrt(jnp.float32(CELL_NODES))
    symmetric = 0.5 * (noise + noise.T)
    diagonal = jax.random.uniform(key_diag, (CELL_NODES,), jnp.float32, 1.5, 2.5)
    return (symmetric + jnp.diag(diagonal)).astype(jnp.bfloat16)


def shard_levels(rng, dims, pieces, least, top_value):
    gain, own = 1.0, jax.random.fold_in(rng, 6)
    for dim, blocks in pieces:
        draws = jnp.exp(jax.random.uniform(jax.random.fold_in(own, dim), (blocks,), jnp.float32, least / len(pieces), top_value / len(pieces)))
        gain = gain * jnp.repeat(draws, dims[dim] // blocks).reshape([-1 if axis == dim else 1 for axis in range(len(dims))])
    return gain


def gaussian(own_key, shape, deviation, bound, shards=(), held_as=jnp.bfloat16):
    drawn = jax.random.normal(own_key, shape, jnp.float32) * deviation
    if len(shards) > 0:
        drawn = shard_levels(own_key, shape, shards, -0.22, 0.18) * drawn
    return jnp.clip(drawn, min=-bound, max=bound).astype(held_as)


def setup_inputs(seed: int = 0) -> dict:
    key_of = jax.random.split(jax.random.key(seed), 9)
    orbitals = gaussian(key_of[0], (DOMAINS, OWN_CAP, BANDS), 1.0, 6.0, ((0, 8), (1, 4)))
    rotation = gaussian(key_of[1], (BANDS, BANDS), BANDS ** -0.5, 0.21875)
    cell_stiffness = draw_cell_stiffness(jax.random.fold_in(key_of[8], 71), 0)
    cell_scale = jnp.clip(jnp.exp(math.log(1.0) - 1.3862944 * jax.random.uniform(key_of[3], (DOMAINS, CELL_CAP), jnp.float32) ** shard_levels(key_of[3], (DOMAINS, CELL_CAP), ((0, 8),), -0.2, 0.2)), 0.25, 1.0)
    potential = jnp.clip(jnp.exp(math.log(2.0) - 2.0794415 * jax.random.uniform(key_of[4], (DOMAINS, OWN_CAP), jnp.float32) ** shard_levels(key_of[4], (DOMAINS, OWN_CAP), ((0, 8),), -0.2, 0.2)), 0.25, 2.0)
    cell_nodes = draw_cell_nodes(jax.random.fold_in(key_of[8], 71), 0)
    send_rows = draw_send_rows(jax.random.fold_in(key_of[8], 71), 0)
    domain_rows = draw_domain_rows(jax.random.fold_in(key_of[8], 71), 0)
    return {"orbitals": orbitals, "rotation": rotation, "cell_stiffness": cell_stiffness, "cell_scale": cell_scale, "potential": potential, "cell_nodes": cell_nodes, "send_rows": send_rows, "domain_rows": domain_rows}


OFFSETS = (1, 8, -8, -1)
CENTER = 5.0
HALF_WIDTH = 5.0


def shift_domains(stacked, offset):
    domain_count = stacked.shape[0]
    padding = [(0, 0)] * stacked.ndim
    if offset > 0:
        padding[0] = (0, offset)
        return jnp.pad(stacked, padding)[offset:offset + domain_count]
    padding[0] = (-offset, 0)
    return jnp.pad(stacked, padding)[:domain_count]


def pick_rows(field, row_lists):
    return jnp.take(field, row_lists.reshape(-1), axis=1, mode="fill", fill_value=0)


def add_rows(result_sum, row_list, arrived):
    return result_sum.at[:, row_list].add(arrived, mode="drop")


def apply_operator(values, stiffness, weights, potential, cell_nodes, send_rows):
    group_width = values.shape[1]
    capacity = values.shape[2]
    picked = jax.vmap(pick_rows)(values, send_rows)
    picked = picked.reshape(DOMAINS, group_width, GROUPS, GHOST_SLOTS)
    ghosts = [shift_domains(picked[:, :, group_pos, :], OFFSETS[group_pos]) for group_pos in range(GROUPS)]
    node_table = jnp.concatenate([values] + ghosts, axis=2)

    def one_domain(domain_table, node_list, cell_weight):
        flat_nodes = node_list.reshape(-1)
        cell_local = jnp.take(domain_table, flat_nodes, axis=1).reshape(group_width * CELL_CAP, CELL_NODES)
        product = jnp.dot(cell_local.astype(jnp.float32), stiffness, preferred_element_type=jnp.float32)
        product = product.reshape(group_width, CELL_CAP, CELL_NODES) * cell_weight[None, :, None]
        empty = jnp.zeros((group_width, domain_table.shape[1]), jnp.float32)
        return empty.at[:, flat_nodes].add(product.reshape(group_width, -1))

    cell_sums = jax.vmap(one_domain)(node_table, cell_nodes, weights)
    result_sum = cell_sums[:, :, :capacity] + potential[:, None, :] * values.astype(jnp.float32)
    ghost_terms = cell_sums[:, :, capacity:]
    for group_pos in range(GROUPS):
        block = ghost_terms[:, :, group_pos * GHOST_SLOTS:(group_pos + 1) * GHOST_SLOTS]
        arrived = shift_domains(block, -OFFSETS[group_pos])
        result_sum = jax.vmap(add_rows)(result_sum, send_rows[:, group_pos], arrived)
    return result_sum


def reference(orbitals, rotation, cell_stiffness, cell_scale, potential, cell_nodes, send_rows, domain_rows):
    capacity = orbitals.shape[1]
    row_index = jnp.arange(capacity, dtype=jnp.int32)
    row_keep = row_index[None, :] < domain_rows[:, None]
    masked = jnp.where(row_keep[:, :, None], orbitals, jnp.zeros_like(orbitals))
    cell_count = (domain_rows - FACE_NODES) // (DEGREE * FACE_NODES)
    cell_live = jnp.arange(CELL_CAP, dtype=jnp.int32)[None, :] < cell_count[:, None]
    weights = jnp.where(cell_live, cell_scale, jnp.zeros_like(cell_scale))
    stiffness = cell_stiffness.astype(jnp.float32)
    flat_rows = masked.reshape(DOMAINS * capacity, BANDS)
    column_sets = rotation.reshape(BANDS, N_BAND, GROUP_WIDTH).transpose(1, 0, 2)

    def one_group(columns):
        rotated = jnp.dot(flat_rows, columns, preferred_element_type=jnp.float32).astype(jnp.bfloat16)
        current = rotated.reshape(DOMAINS, capacity, GROUP_WIDTH).transpose(0, 2, 1)
        previous = current
        for filter_step in range(FILTER_STEPS):
            applied = apply_operator(current, stiffness, weights, potential, cell_nodes, send_rows)
            shifted = applied - CENTER * current.astype(jnp.float32)
            if filter_step == 0:
                following = shifted / HALF_WIDTH
            else:
                following = 2.0 * shifted / HALF_WIDTH - previous.astype(jnp.float32)
            previous, current = current, following.astype(jnp.bfloat16)
        return current

    filtered = lax.map(one_group, column_sets)
    return filtered.transpose(1, 3, 0, 2).reshape(DOMAINS, capacity, BANDS)
```

```python
import jax
import jax.numpy as jnp
from jax import lax
from jax.sharding import PartitionSpec as P

DEGREE = 8
FILTER_STEPS = 3
FACE_NODES = 81

OFFSETS = (1, 8, -8, -1)
CENTER = 5.0
HALF_WIDTH = 5.0


def round_up(value, multiple):
    return -(-value // multiple) * multiple


def swap(value, first):
    domains = lax.axis_size("dom")
    pairs = []
    for low in range(first, domains - 1, 2):
        pairs += [(low, low + 1), (low + 1, low)]
    return lax.ppermute(value, "dom", pairs)


def shift(value, by):
    domains = lax.axis_size("dom")
    pairs = [(i, i + by) for i in range(domains) if 0 <= i + by < domains]
    return lax.ppermute(value, "dom", pairs)


def far_groups(domains):
    return [g for g, offset in enumerate(OFFSETS) if abs(offset) > 1 and abs(offset) < domains]


def exchange(blocks, to_owner):
    far = far_groups(lax.axis_size("dom"))
    out = [swap(blocks[0], 0), swap(blocks[1], 1)]
    for block, group in zip(blocks[2:], far):
        out.append(shift(block, OFFSETS[group] if to_owner else -OFFSETS[group]))
    return out


def dot(a, b, contract):
    return lax.dot_general(a, b, (contract, ((), ())), preferred_element_type=jnp.float32)


def shards(
    orbitals, rotation, cell_stiffness, cell_scale, potential, cell_nodes, send_rows, domain_rows
):
    bf16 = jnp.bfloat16
    domains = lax.axis_size("dom")
    domain = lax.axis_index("dom")
    row_piece = orbitals[0]
    piece_rows = row_piece.shape[0]
    own_rows = domain_rows[0]
    first_row = lax.axis_index("band") * piece_rows
    row_keep = first_row + jnp.arange(piece_rows, dtype=jnp.int32) < own_rows
    row_piece = jnp.where(row_keep[:, None], row_piece, jnp.zeros_like(row_piece))
    rotated = dot(row_piece, rotation, ((1,), (0,))).astype(bf16)
    current = lax.all_to_all(rotated, "band", split_axis=1, concat_axis=0, tiled=True)

    capacity = potential.shape[1]
    cells, nodes = cell_nodes.shape[1:]
    slots = send_rows.shape[2]
    nodes_pad = round_up(nodes, 256)
    slots_pad = round_up(slots, 64)
    far = far_groups(domains)
    blocks = 2 + len(far)
    even = domain % 2 == 0
    send_lists = [
        jnp.where(even, send_rows[0, 3], send_rows[0, 0]),
        jnp.where(even, send_rows[0, 0], send_rows[0, 3]),
    ] + [send_rows[0, g] for g in far]
    send_list = jnp.stack(send_lists)
    send_list = jnp.pad(send_list, ((0, 0), (0, slots_pad - slots)), constant_values=capacity).reshape(-1)
    group = (cell_nodes[0] - capacity) // slots
    slot = (cell_nodes[0] - capacity) % slots
    block = jnp.where((group == 0) == even, 0, 1)
    for pos, g in enumerate(far):
        block = jnp.where(group == g, 2 + pos, block)
    ghost_index = block * slots_pad + slot
    is_own = cell_nodes[0] < capacity
    pad = ((0, 0), (0, nodes_pad - nodes))
    own_index = jnp.pad(jnp.where(is_own, cell_nodes[0], -1), pad, constant_values=-1).reshape(-1)
    ghost_index = jnp.pad(jnp.where(is_own, -1, ghost_index), pad, constant_values=-1).reshape(-1)
    own_iota = jnp.arange(capacity, dtype=jnp.int32)
    ghost_iota = jnp.arange(blocks * slots_pad, dtype=jnp.int32)
    pick_own = (own_index[:, None] == own_iota[None, :]).astype(bf16)
    pick_ghost = (ghost_index[:, None] == ghost_iota[None, :]).astype(bf16)
    pick_send = (send_list[:, None] == own_iota[None, :]).astype(bf16)
    stiffness = jnp.pad(cell_stiffness, ((0, nodes_pad - nodes), (0, nodes_pad - nodes)))

    cell_total = (own_rows - FACE_NODES) // (DEGREE * FACE_NODES)
    cell_live = jnp.arange(cell_scale.shape[1], dtype=jnp.int32) < cell_total
    cell_weight = jnp.where(cell_live, cell_scale[0], jnp.zeros_like(cell_scale[0]))
    node_potential = potential[0][:, None]
    previous = current
    width = current.shape[1]
    for filter_step in range(FILTER_STEPS):
        picked = dot(pick_send, current, ((1,), (0,))).astype(bf16).reshape(blocks, slots_pad, width)
        ghosts = jnp.concatenate(exchange([picked[b] for b in range(blocks)], False), axis=0)
        local = dot(pick_own, current, ((1,), (0,))) + dot(pick_ghost, ghosts, ((1,), (0,)))
        local = local.astype(bf16).reshape(cells, nodes_pad, width)
        product = jnp.stack([dot(stiffness, local[c], ((0,), (0,))) for c in range(cells)])
        product = (product * cell_weight[:, None, None]).astype(bf16).reshape(-1, width)
        terms = dot(pick_ghost, product, ((0,), (0,))).astype(bf16).reshape(blocks, slots_pad, width)
        arrived = jnp.concatenate(exchange([terms[b] for b in range(blocks)], True), axis=0)
        applied = dot(pick_own, product, ((0,), (0,))) + dot(pick_send, arrived, ((0,), (0,)))
        values = current.astype(jnp.float32)
        shifted = applied + (node_potential - CENTER) * values
        if filter_step == 0:
            following = shifted / HALF_WIDTH
        else:
            following = 2.0 * shifted / HALF_WIDTH - previous.astype(jnp.float32)
        previous, current = current, following.astype(bf16)
    return current[None]


def solution(mesh):
    return jax.shard_map(
        shards,
        mesh=mesh,
        in_specs=(
            P("dom", "band", None),
            P(),
            P(),
            P("dom", None),
            P("dom", None),
            P("dom", None, None),
            P("dom", None, None),
            P("dom"),
        ),
        out_specs=P("dom", None, "band"),
        check_vma=False,
    )
```

```python
import functools

import jax
import jax.numpy as jnp
from jax import lax
from jax.experimental import pallas as pl
from jax.experimental.pallas import tpu as pltpu
from jax.sharding import PartitionSpec as P

DEGREE = 8
FILTER_STEPS = 3
FACE_NODES = 81

OFFSETS = (1, 8, -8, -1)
CENTER = 5.0
HALF_WIDTH = 5.0
BF16 = jnp.bfloat16
F32 = jnp.float32
VMEM = pl.BlockSpec(memory_space=pltpu.VMEM)
SMEM = pl.BlockSpec(memory_space=pltpu.SMEM)


def round_up(value, multiple):
    return -(-value // multiple) * multiple


def swap(value, first):
    domains = lax.axis_size("dom")
    pairs = []
    for low in range(first, domains - 1, 2):
        pairs += [(low, low + 1), (low + 1, low)]
    return lax.ppermute(value, "dom", pairs)


def shift(value, by):
    domains = lax.axis_size("dom")
    pairs = [(i, i + by) for i in range(domains) if 0 <= i + by < domains]
    return lax.ppermute(value, "dom", pairs)


def far_groups(domains):
    return [g for g, offset in enumerate(OFFSETS) if abs(offset) > 1 and abs(offset) < domains]


def exchange(blocks, to_owner):
    far = far_groups(lax.axis_size("dom"))
    out = [swap(blocks[0], 0), swap(blocks[1], 1)]
    for block, group in zip(blocks[2:], far):
        out.append(shift(block, OFFSETS[group] if to_owner else -OFFSETS[group]))
    return out


def call(kernel, out_shape, args, flops, scalars=0, scratch=()):
    outs = out_shape if isinstance(out_shape, (tuple, list)) else (out_shape,)
    size = sum(a.size * a.dtype.itemsize for a in list(args) + list(outs))
    return pl.pallas_call(
        kernel,
        out_shape=out_shape,
        in_specs=[SMEM] * scalars + [VMEM] * (len(args) - scalars),
        out_specs=jax.tree.map(lambda _: VMEM, out_shape),
        scratch_shapes=list(scratch),
        cost_estimate=pl.CostEstimate(flops=flops, bytes_accessed=size, transcendentals=0),
        compiler_params=pltpu.CompilerParams(vmem_limit_bytes=24 << 20),
    )(*args)


def shape(dims, dtype):
    return jax.ShapeDtypeStruct(dims, dtype)


def mm(a, b):
    return jnp.dot(a, b, preferred_element_type=F32)


def mm_nt(a, b):
    return lax.dot_general(a, b, (((1,), (1,)), ((), ())), preferred_element_type=F32)


def rows_hot(index, first, count):
    rows = lax.broadcasted_iota(jnp.int32, (count, index.shape[1]), 0) + first
    return (rows == index).astype(BF16)


def steps(total, size):
    return [(i, min(size, total - i)) for i in range(0, total, size)]


def rotate_kernel(scalars, piece, rotation, out):
    width = out.shape[1]
    rotated = lax.dot_general(
        rotation[...], piece[...], (((0,), (0,)), ((), ())), preferred_element_type=F32
    )
    rows = lax.broadcasted_iota(jnp.int32, rotated.shape, 1) + scalars[0]
    rotated = jnp.where(rows < scalars[1], rotated, 0.0)
    for group in range(out.shape[0]):
        out[group] = rotated[group * width : (group + 1) * width, :].astype(BF16)


def couple_kernel(capacity, weight, node_row, stiffness, to_ghost, to_own, *locals_):
    nodes = stiffness.shape[0]
    blocks, slots = to_own.shape[:2]
    for block in range(blocks):
        local = locals_[block]
        for cell in range(weight.shape[0]):
            picks = rows_hot(node_row[:, cell * nodes : (cell + 1) * nodes], capacity + block * slots, slots)
            product = mm(picks, stiffness[...]) * weight[cell]
            local[:, cell * nodes : (cell + 1) * nodes] = product.astype(BF16)
        for other in range(blocks):
            picks = rows_hot(node_row[...], capacity + other * slots, slots)
            to_ghost[block, other] = mm_nt(local[...], picks).astype(BF16)
    for i, n in steps(capacity, 256):
        picks = rows_hot(node_row[...], i, n)
        for block in range(blocks):
            to_own[block, :, i : i + n] = mm_nt(locals_[block][...], picks).astype(BF16)


def pick_rows(send_row, values, outs):
    for block, out in enumerate(outs):
        picks = rows_hot(send_row[block : block + 1, :], 0, values.shape[1])
        out[...] = mm(values[...], picks).astype(BF16)


def join_kernel(send_row, pieces, values, *outs):
    values[...] = jnp.concatenate([pieces[p] for p in range(pieces.shape[0])], axis=1)
    pick_rows(send_row, values, outs)


def cells_kernel(weight, node_row, stiffness, values, product, terms, local):
    capacity = values.shape[1]
    nodes = stiffness.shape[0]
    blocks, _, slots = terms.shape
    for cell in range(weight.shape[0]):
        first = cell * nodes
        for i, n in steps(nodes, 256):
            picks = rows_hot(node_row[:, first + i : first + i + n], 0, capacity)
            local[:, i : i + n] = mm(values[...], picks).astype(BF16)
        result = mm(local[...], stiffness[...]) * weight[cell]
        product[:, first : first + nodes] = result.astype(BF16)
    for block in range(blocks):
        terms[block] = mm_nt(product[...], rows_hot(node_row[...], capacity + block * slots, slots))


def ghost_kernel(terms, to_ghost, *refs):
    blocks = terms.shape[0]
    arrived, outs = refs[:blocks], refs[blocks:]
    for block in range(blocks):
        total = terms[block]
        for other in range(blocks):
            total = total + mm(arrived[other][...], to_ghost[other, block])
        outs[block][...] = total.astype(BF16)


def own_kernel(node_row, product, to_own, *refs):
    arrived, out = refs[:-1], refs[-1]
    for i, n in steps(out.shape[1], 256):
        total = mm_nt(product[...], rows_hot(node_row[...], i, n))
        for block, ghost in enumerate(arrived):
            total = total + mm(ghost[...], to_own[block, :, i : i + n])
        out[:, i : i + n] = total


def update_kernel(blocks, first_step, last_step, send_row, potential, total, values, *refs):
    refs = list(refs)
    previous = None if first_step else refs.pop(0)
    arrived, out, picked = refs[:blocks], refs[blocks], refs[blocks + 1 :]
    for i, n in steps(out.shape[1], 256):
        at = slice(i, i + n)
        applied = total[:, at]
        for block in range(blocks):
            applied = applied + mm_nt(arrived[block][...], rows_hot(send_row[block : block + 1, :], i, n))
        shifted = applied + (potential[:, at] - CENTER) * values[:, at].astype(F32)
        if first_step:
            following = shifted * (1.0 / HALF_WIDTH)
        else:
            following = shifted * (2.0 / HALF_WIDTH) - previous[:, at].astype(F32)
        out[:, at] = following.astype(BF16)
    if not last_step:
        pick_rows(send_row, out, picked)


def shards(
    orbitals, rotation, cell_stiffness, cell_scale, potential, cell_nodes, send_rows, domain_rows
):
    domains = lax.axis_size("dom")
    bands = lax.axis_size("band")
    domain = lax.axis_index("dom")
    row_piece = orbitals[0]
    piece_rows, columns = row_piece.shape
    own_rows = domain_rows[0]
    width = columns // bands
    first_row = lax.axis_index("band") * piece_rows
    rotated = call(
        rotate_kernel,
        shape((bands, width, piece_rows), BF16),
        (jnp.stack([first_row, own_rows]).astype(jnp.int32), row_piece.T, rotation),
        2 * piece_rows * columns * columns,
        scalars=1,
    )
    pieces = lax.all_to_all(rotated, "band", split_axis=0, concat_axis=0, tiled=True)

    capacity = potential.shape[1]
    cells, nodes = cell_nodes.shape[1:]
    slots = send_rows.shape[2]
    nodes_pad = round_up(nodes, 256)
    slots_pad = round_up(slots, 16)
    far = far_groups(domains)
    blocks = 2 + len(far)
    ghosts = blocks * slots_pad
    even = domain % 2 == 0
    send_lists = [
        jnp.where(even, send_rows[0, 3], send_rows[0, 0]),
        jnp.where(even, send_rows[0, 0], send_rows[0, 3]),
    ] + [send_rows[0, g] for g in far]
    send_row = jnp.pad(
        jnp.stack(send_lists), ((0, 0), (0, slots_pad - slots)), constant_values=capacity
    )
    group = (cell_nodes[0] - capacity) // slots
    slot = (cell_nodes[0] - capacity) % slots
    block = jnp.where((group == 0) == even, 0, 1)
    for pos, g in enumerate(far):
        block = jnp.where(group == g, 2 + pos, block)
    ghost_index = capacity + block * slots_pad + slot
    node_list = jnp.where(cell_nodes[0] < capacity, cell_nodes[0], ghost_index)
    node_list = jnp.pad(
        node_list, ((0, 0), (0, nodes_pad - nodes)), constant_values=capacity + ghosts
    ).reshape(-1)
    node_row = node_list[None, :]
    stiffness = jnp.pad(cell_stiffness, ((0, nodes_pad - nodes), (0, nodes_pad - nodes)))

    cell_total = (own_rows - FACE_NODES) // (DEGREE * FACE_NODES)
    cell_live = jnp.arange(cell_scale.shape[1], dtype=jnp.int32) < cell_total
    weight = jnp.where(cell_live, cell_scale[0], jnp.zeros_like(cell_scale[0]))

    local_rows = cells * nodes_pad
    cell_flops = 2 * local_rows * nodes_pad
    to_ghost, to_own = call(
        functools.partial(couple_kernel, capacity),
        (
            shape((blocks, blocks, slots_pad, slots_pad), BF16),
            shape((blocks, slots_pad, capacity), BF16),
        ),
        (weight, node_row, stiffness),
        (cell_flops + 2 * local_rows * (ghosts + capacity)) * ghosts,
        scalars=1,
        scratch=[pltpu.VMEM((slots_pad, local_rows), BF16)] * blocks,
    )
    block_shapes = (shape((width, slots_pad), BF16),) * blocks
    current, *picked = call(
        join_kernel,
        (shape((width, capacity), BF16),) + block_shapes,
        (send_row, pieces),
        2 * ghosts * capacity * width,
    )
    previous = None
    for filter_step in range(FILTER_STEPS):
        last = filter_step == FILTER_STEPS - 1
        arrived = exchange(picked, False)
        product, terms = call(
            cells_kernel,
            (shape((width, local_rows), BF16), shape((blocks, width, slots_pad), F32)),
            (weight, node_row, stiffness, current),
            (cell_flops + 2 * local_rows * (capacity + ghosts)) * width,
            scalars=1,
            scratch=[pltpu.VMEM((width, nodes_pad), BF16)],
        )
        sums = call(
            ghost_kernel, block_shapes, (terms, to_ghost, *arrived), 2 * ghosts * ghosts * width
        )
        returned = exchange(sums, True)
        total = call(
            own_kernel,
            shape((width, capacity), F32),
            (node_row, product, to_own, *arrived),
            2 * capacity * (local_rows + ghosts) * width,
        )
        operands = [send_row, potential, total, current]
        if previous is not None:
            operands.append(previous)
        following, *picked = call(
            functools.partial(update_kernel, blocks, previous is None, last),
            (shape((width, capacity), BF16),) + (() if last else block_shapes),
            (*operands, *returned),
            4 * capacity * ghosts * width,
        )
        previous, current = current, following
    return current.T[None]


def solution(mesh):
    return jax.shard_map(
        shards,
        mesh=mesh,
        in_specs=(
            P("dom", "band", None),
            P(),
            P(),
            P("dom", None),
            P("dom", None),
            P("dom", None, None),
            P("dom", None, None),
            P("dom"),
        ),
        out_specs=P("dom", None, "band"),
        check_vma=False,
    )
```

```python
import functools

import jax
import jax.numpy as jnp
from jax import lax
from jax.experimental import pallas as pl
from jax.experimental.pallas import tpu as pltpu
from jax.sharding import PartitionSpec as P

DEGREE = 8
FILTER_STEPS = 3
FACE_NODES = 81

OFFSETS = (1, 8, -8, -1)
CENTER = 5.0
HALF_WIDTH = 5.0
BF16 = jnp.bfloat16
F32 = jnp.float32
VMEM = pl.BlockSpec(memory_space=pltpu.VMEM)
ANY = pl.BlockSpec(memory_space=pl.ANY)
LANES = 128
ROTATE_VMEM = 56 << 20
HEAD = 768


def round_up(value, multiple):
    return -(-value // multiple) * multiple


def swap(value, first):
    domains = lax.axis_size("dom")
    pairs = []
    for low in range(first, domains - 1, 2):
        pairs += [(low, low + 1), (low + 1, low)]
    return lax.ppermute(value, "dom", pairs)


def shift(value, by):
    domains = lax.axis_size("dom")
    pairs = [(i, i + by) for i in range(domains) if 0 <= i + by < domains]
    return lax.ppermute(value, "dom", pairs)


def far_groups(domains):
    return [g for g, offset in enumerate(OFFSETS) if abs(offset) > 1 and abs(offset) < domains]


def exchange(blocks, to_owner):
    out = [swap(blocks[0], 1)]
    for block, group in zip(blocks[1:], far_groups(lax.axis_size("dom"))):
        out.append(shift(block, OFFSETS[group] if to_owner else -OFFSETS[group]))
    return out


def call(kernel, out_shape, args, flops, scratch=(), in_specs=None, vmem=24 << 20):
    outs = out_shape if isinstance(out_shape, (tuple, list)) else (out_shape,)
    size = sum(a.size * a.dtype.itemsize for a in list(args) + list(outs))
    return pl.pallas_call(
        kernel,
        out_shape=out_shape,
        in_specs=in_specs or [VMEM] * len(args),
        out_specs=jax.tree.map(lambda _: VMEM, out_shape),
        scratch_shapes=list(scratch),
        cost_estimate=pl.CostEstimate(flops=flops, bytes_accessed=size, transcendentals=0),
        compiler_params=pltpu.CompilerParams(vmem_limit_bytes=vmem),
    )(*args)


def shape(dims, dtype):
    return jax.ShapeDtypeStruct(dims, dtype)


def mm(a, b):
    return jnp.dot(a, b, preferred_element_type=F32)


def mm_nt(a, b):
    return lax.dot_general(a, b, (((1,), (1,)), ((), ())), preferred_element_type=F32)


def rows_hot(index, first, count):
    rows = lax.broadcasted_iota(jnp.int32, (count, index.shape[1]), 0) + first
    return (rows == index).astype(BF16)


def steps(total, size):
    return [(i, min(size, total - i)) for i in range(0, total, size)]


def rotate_kernel(piece, rotation, *refs):
    outs, (piece_held, rotation_held, groups, sems) = refs[:-4], refs[-4:]
    copies = (
        pltpu.make_async_copy(rotation, rotation_held, sems.at[0]),
        pltpu.make_async_copy(piece, piece_held, sems.at[1]),
    )
    for copy in copies:
        copy.start()
    for copy in copies:
        copy.wait()
    rotated = lax.dot_general(
        rotation_held[...], piece_held[...], (((0,), (0,)), ((), ())), preferred_element_type=F32
    )
    width = groups.shape[1]
    for group in range(groups.shape[0]):
        groups[group] = rotated[group * width : (group + 1) * width, :].astype(BF16)
    mine = lax.axis_index("band")
    for k, out in enumerate(outs):
        out[...] = groups[mine ^ k]


def columns_hot(index, capacity, hot):
    turned = jnp.broadcast_to(index, (LANES, index.shape[1])).T
    for i, n in steps(capacity, LANES):
        lanes = lax.broadcasted_iota(jnp.int32, (turned.shape[0], n), 1) + i
        hot[:, i : i + n] = (turned[:, :n] == lanes).astype(BF16)


def couple_kernel(capacity, weight, node_row, stiffness, to_ghost, to_own, scatter, local):
    nodes = stiffness.shape[0]
    ghosts = to_own.shape[0]
    slots = to_ghost.shape[2]
    for i, n in steps(node_row.shape[1], nodes):
        picks = rows_hot(node_row[:, i : i + n], capacity, ghosts)
        local[:, i : i + n] = (mm(picks, stiffness[...]) * weight[:, i : i + n]).astype(BF16)
    columns_hot(node_row[...], capacity, scatter)
    for block in range(to_ghost.shape[0]):
        picks = rows_hot(node_row[...], capacity + block * slots, slots)
        to_ghost[block] = mm_nt(local[...], picks).astype(BF16)
    for i, n in steps(capacity, 256):
        to_own[:, i : i + n] = mm(local[...], scatter[:, i : i + n]).astype(BF16)


def pick_rows(send_row, block, values, out):
    picks = rows_hot(send_row[block : block + 1, :], 0, values.shape[1])
    out[...] = mm(values[...], picks).astype(BF16)


def join_kernel(send_row, keep, after, *refs):
    bands = refs[-1].shape[0]
    pieces, (values, near_picked, held) = refs[:bands], refs[bands:]
    mine = lax.axis_index("band")
    for k, piece in enumerate(pieces):
        held[mine ^ k] = piece[...]
    joined = jnp.concatenate([held[p] for p in range(bands)], axis=1)
    values[...] = jnp.where(keep[...] > 0, joined.astype(F32), 0.0).astype(BF16)
    pick_rows(send_row, 0, values, near_picked)


def terms_kernel(send_row, to_own, values, terms, *picked):
    slots = terms.shape[2]
    for block, out in enumerate(picked):
        pick_rows(send_row, block + 1, values, out)
    for block in range(terms.shape[0]):
        terms[block] = mm_nt(values[...], to_own[block * slots : (block + 1) * slots, :])


def cells_kernel(first_step, weight, node_row, stiffness, scatter, potential, values, after, *refs):
    refs = list(refs)
    previous = None if first_step else refs.pop(0)
    product, head, *locals_ = refs
    capacity = values.shape[1]
    nodes = stiffness.shape[0]
    parts = steps(product.shape[1], nodes)
    for (i, n), local in zip(parts, locals_):
        local[...] = mm(values[...], rows_hot(node_row[:, i : i + n], 0, capacity)).astype(BF16)
    for (i, n), local in zip(parts, locals_):
        product[:, i : i + n] = (mm(local[...], stiffness[...]) * weight[:, i : i + n]).astype(BF16)
    for i, n in steps(head.shape[1], 256):
        at = slice(i, i + n)
        sums = mm(product[...], scatter[:, at])
        head[:, at] = own_columns(first_step, at, sums, potential, values, previous)


def ghost_sum(block, terms, to_ghost, arrived):
    slots = terms.shape[2]
    total = terms[block]
    for other, values in arrived:
        total = total + mm(values, to_ghost[block, other * slots : (other + 1) * slots, :])
    return total.astype(BF16)


def ghost_kernel(terms, to_ghost, *refs):
    blocks = terms.shape[0]
    arrived = [(other, refs[other][...]) for other in range(blocks)]
    for block in range(blocks):
        refs[blocks + block][...] = ghost_sum(block, terms, to_ghost, arrived)


def parcel_kernel(terms, to_ghost, near_ghosts, far_picked, parcel):
    width, slots = far_picked.shape
    sums = ghost_sum(1, terms, to_ghost, [(0, near_ghosts[...])])
    parcel[:width, :] = jnp.concatenate([far_picked[...], sums], axis=1)
    if parcel.shape[0] > width:
        parcel[width:, :] = jnp.zeros((parcel.shape[0] - width, 2 * slots), BF16)
        first = parcel.shape[0] - slots
        parcel[first:, :slots] = to_ghost[1, slots : 2 * slots, :]


def near_kernel(terms, to_ghost, near_ghosts, parcel, after, out):
    width, slots = out.shape
    arrived = [(0, near_ghosts[...]), (1, parcel[:width, :slots])]
    out[...] = ghost_sum(0, terms, to_ghost, arrived)


def scale_of(first_step):
    return (1.0 if first_step else 2.0) / HALF_WIDTH


def own_columns(first_step, at, sums, potential, values, previous):
    shifted = sums + (potential[:, at] - CENTER) * values[:, at].astype(F32)
    result = shifted * scale_of(first_step)
    return result if first_step else result - previous[:, at].astype(F32)


def own_kernel(first_step, product, scatter, to_own, potential, values, head, *refs):
    refs = list(refs)
    previous = None if first_step else refs.pop(0)
    arrived, out = refs[:-1], refs[-1]
    ghosts = jnp.concatenate([ghost[...] for ghost in arrived], axis=1)
    for i, n in steps(out.shape[1], 256):
        at = slice(i, i + n)
        sums = mm(ghosts, to_own[:, at])
        if i < head.shape[1]:
            out[:, at] = head[:, at] + sums * scale_of(first_step)
        else:
            sums = sums + mm(product[...], scatter[:, at])
            out[:, at] = own_columns(first_step, at, sums, potential, values, previous)


def paired_own_kernel(
    first_step, product, scatter, to_own, potential, values, head, send_row, near_ghosts, far_picked, parcel, first_parcel, *refs
):
    previous, out = (None if first_step else refs[0]), refs[-1]
    width, slots = far_picked.shape
    ghosts = jnp.concatenate([near_ghosts[...], parcel[:width, :slots]], axis=1)
    coupling = first_parcel[first_parcel.shape[0] - slots :, :slots]
    returned = parcel[:width, slots:].astype(F32) + mm(far_picked[...], coupling)
    returned = returned.astype(BF16)
    for i, n in steps(out.shape[1], 256):
        at = slice(i, i + n)
        sums = mm(ghosts, to_own[:, at]) + mm_nt(returned, rows_hot(send_row[1:2, :], i, n))
        if i < head.shape[1]:
            out[:, at] = head[:, at] + sums * scale_of(first_step)
        else:
            sums = sums + mm(product[...], scatter[:, at])
            out[:, at] = own_columns(first_step, at, sums, potential, values, previous)


def update_kernel(blocks, first_step, last_step, send_row, total, *refs):
    arrived, out, picked = refs[:blocks], refs[blocks], refs[blocks + 1 :]
    for i, n in steps(out.shape[1], 256):
        at = slice(i, i + n)
        added = 0.0
        for block in range(blocks):
            added = added + mm_nt(arrived[block][...], rows_hot(send_row[block : block + 1, :], i, n))
        out[:, at] = (total[:, at] + added * scale_of(first_step)).astype(BF16)
    if not last_step:
        pick_rows(send_row, 0, out, picked[0])


def shards(
    orbitals, rotation, cell_stiffness, cell_scale, potential, cell_nodes, send_rows, domain_rows
):
    domains = lax.axis_size("dom")
    bands = lax.axis_size("band")
    domain = lax.axis_index("dom")
    row_piece = orbitals[0]
    piece_rows, columns = row_piece.shape
    own_rows = domain_rows[0]
    width = columns // bands
    piece_shapes = (shape((width, piece_rows), BF16),) * bands
    pieces = list(call(
        rotate_kernel,
        piece_shapes,
        (row_piece.T, rotation),
        2 * piece_rows * columns * columns,
        scratch=[
            pltpu.VMEM((columns, piece_rows), BF16),
            pltpu.VMEM((columns, columns), BF16),
            pltpu.VMEM((bands, width, piece_rows), BF16),
            pltpu.SemaphoreType.DMA((2,)),
        ],
        in_specs=[ANY, ANY],
        vmem=ROTATE_VMEM,
    ))
    for k in reversed(range(1, bands)):
        pieces[k] = lax.ppermute(pieces[k], "band", [(i, i ^ k) for i in range(bands)])

    capacity = potential.shape[1]
    cells, nodes = cell_nodes.shape[1:]
    slots = send_rows.shape[2]
    nodes_pad = round_up(nodes, 256)
    slots_pad = round_up(slots, 16)
    far = far_groups(domains)
    blocks = 2 + len(far)
    ghosts = blocks * slots_pad
    even = domain % 2 == 0
    send_lists = [
        jnp.where(even, send_rows[0, 3], send_rows[0, 0]),
        jnp.where(even, send_rows[0, 0], send_rows[0, 3]),
    ] + [send_rows[0, g] for g in far]
    send_row = jnp.pad(
        jnp.stack(send_lists), ((0, 0), (0, slots_pad - slots)), constant_values=capacity
    )
    group = (cell_nodes[0] - capacity) // slots
    slot = (cell_nodes[0] - capacity) % slots
    block = jnp.where((group == 0) == even, 0, 1)
    for pos, g in enumerate(far):
        block = jnp.where(group == g, 2 + pos, block)
    ghost_index = capacity + block * slots_pad + slot
    node_list = jnp.where(cell_nodes[0] < capacity, cell_nodes[0], ghost_index)
    node_list = jnp.pad(
        node_list, ((0, 0), (0, nodes_pad - nodes)), constant_values=capacity + ghosts
    ).reshape(-1)
    node_row = node_list[None, :]
    stiffness = jnp.pad(cell_stiffness, ((0, nodes_pad - nodes), (0, nodes_pad - nodes)))

    cell_total = (own_rows - FACE_NODES) // (DEGREE * FACE_NODES)
    cell_live = jnp.arange(cell_scale.shape[1], dtype=jnp.int32) < cell_total
    weight = jnp.where(cell_live, cell_scale[0], jnp.zeros_like(cell_scale[0]))
    weight = jnp.repeat(weight, nodes_pad)[None, :]

    local_rows = cells * nodes_pad
    cell_flops = 2 * local_rows * nodes_pad
    to_ghost, to_own, scatter = call(
        functools.partial(couple_kernel, capacity),
        (
            shape((blocks, ghosts, slots_pad), BF16),
            shape((ghosts, capacity), BF16),
            shape((local_rows, capacity), BF16),
        ),
        (weight, node_row, stiffness),
        (cell_flops + 2 * local_rows * (ghosts + capacity)) * ghosts,
        scratch=[pltpu.VMEM((ghosts, local_rows), BF16)],
    )
    block_shape = shape((width, slots_pad), BF16)
    keep = (jnp.arange(capacity, dtype=jnp.int32) < own_rows).astype(jnp.int32)[None, :]
    current, near_picked = call(
        join_kernel,
        (shape((width, capacity), BF16), block_shape),
        (send_row, keep, to_ghost, *pieces),
        2 * slots_pad * capacity * width,
        scratch=[pltpu.VMEM((bands, width, piece_rows), BF16)],
        in_specs=[VMEM, VMEM, ANY] + [VMEM] * bands,
    )
    head_columns = min(HEAD, capacity)
    previous = None
    parcel_rows = round_up(width, 16) + slots_pad
    first_parcel = None
    for filter_step in range(FILTER_STEPS):
        first, last = filter_step == 0, filter_step == FILTER_STEPS - 1
        near = swap(near_picked, 0)
        terms, *picked = call(
            terms_kernel,
            (shape((blocks, width, slots_pad), F32),) + (block_shape,) * (blocks - 1),
            (send_row, to_own, current),
            4 * ghosts * capacity * width,
        )
        if far:
            arrived = [near, *exchange(picked, False)]
            ready = terms
        else:
            parcel = call(
                parcel_kernel,
                shape((parcel_rows if first else width, 2 * slots_pad), BF16),
                (terms, to_ghost, near, picked[0]),
                2 * slots_pad * slots_pad * width,
            )
            ready = parcel
            parcel = swap(parcel, 1)
            first_parcel = parcel if first else first_parcel
        history = () if first else (previous,)
        product, head = call(
            functools.partial(cells_kernel, first),
            (shape((width, local_rows), BF16), shape((width, head_columns), F32)),
            (weight, node_row, stiffness, scatter, potential, current, ready, *history),
            (cell_flops + 2 * local_rows * (capacity + head_columns)) * width,
            scratch=[pltpu.VMEM((width, nodes_pad), BF16)] * cells,
            in_specs=[VMEM] * 6 + [ANY] + [VMEM] * len(history),
        )
        own_flops = 2 * ((capacity - head_columns) * local_rows + capacity * ghosts) * width
        own_operands = (product, scatter, to_own, potential, current, head)
        if far:
            sums = call(
                ghost_kernel,
                (block_shape,) * blocks,
                (terms, to_ghost, *arrived),
                2 * ghosts * ghosts * width,
            )
            returned = [swap(sums[0], 0), *exchange(sums[1:], True)]
            total = call(
                functools.partial(own_kernel, first),
                shape((width, capacity), F32),
                (*own_operands, *history, *arrived),
                own_flops,
            )
        else:
            sums = call(
                near_kernel,
                block_shape,
                (terms, to_ghost, near, parcel, head),
                2 * ghosts * slots_pad * width,
                in_specs=[VMEM] * 4 + [ANY],
            )
            returned = [swap(sums, 0)]
            total = call(
                functools.partial(paired_own_kernel, first),
                shape((width, capacity), F32),
                (*own_operands, send_row, near, picked[0], parcel, first_parcel, *history),
                own_flops,
            )
        following, *near_next = call(
            functools.partial(update_kernel, len(returned), first, last),
            (shape((width, capacity), BF16),) + (() if last else (block_shape,)),
            (send_row, total, *returned),
            2 * capacity * (ghosts + slots_pad * len(returned)) * width,
        )
        previous, current = current, following
        near_picked = near_next[0] if near_next else None
    return current.T[None]


def solution(mesh):
    return jax.shard_map(
        shards,
        mesh=mesh,
        in_specs=(
            P("dom", "band", None),
            P(),
            P(),
            P("dom", None),
            P("dom", None),
            P("dom", None, None),
            P("dom", None, None),
            P("dom"),
        ),
        out_specs=P("dom", None, "band"),
        check_vma=False,
    )
```

```python
import functools

import jax
import jax.numpy as jnp
from jax import lax
from jax.experimental import pallas as pl
from jax.experimental.pallas import tpu as pltpu
from jax.sharding import PartitionSpec as P

DEGREE = 8
FILTER_STEPS = 3
FACE_NODES = 81

OFFSETS = (1, 8, -8, -1)
CENTER = 5.0
HALF_WIDTH = 5.0
BF16 = jnp.bfloat16
F32 = jnp.float32
VMEM = pl.BlockSpec(memory_space=pltpu.VMEM)
ANY = pl.BlockSpec(memory_space=pl.ANY)
LANES = 128
ROTATE_VMEM = 56 << 20


def round_up(value, multiple):
    return -(-value // multiple) * multiple


def swap(value, first):
    domains = lax.axis_size("dom")
    pairs = []
    for low in range(first, domains - 1, 2):
        pairs += [(low, low + 1), (low + 1, low)]
    return lax.ppermute(value, "dom", pairs)


def shift(value, by):
    domains = lax.axis_size("dom")
    pairs = [(i, i + by) for i in range(domains) if 0 <= i + by < domains]
    return lax.ppermute(value, "dom", pairs)


def far_groups(domains):
    return [g for g, offset in enumerate(OFFSETS) if abs(offset) > 1 and abs(offset) < domains]


def exchange(blocks, to_owner):
    out = [swap(blocks[0], 1)]
    for block, group in zip(blocks[1:], far_groups(lax.axis_size("dom"))):
        out.append(shift(block, OFFSETS[group] if to_owner else -OFFSETS[group]))
    return out


def call(kernel, out_shape, args, flops, scratch=(), in_specs=None, out_specs=None, vmem=24 << 20):
    outs = out_shape if isinstance(out_shape, (tuple, list)) else (out_shape,)
    size = sum(a.size * a.dtype.itemsize for a in list(args) + list(outs))
    return pl.pallas_call(
        kernel,
        out_shape=out_shape,
        in_specs=in_specs or [VMEM] * len(args),
        out_specs=out_specs or jax.tree.map(lambda _: VMEM, out_shape),
        scratch_shapes=list(scratch),
        cost_estimate=pl.CostEstimate(flops=flops, bytes_accessed=size, transcendentals=0),
        compiler_params=pltpu.CompilerParams(vmem_limit_bytes=vmem),
    )(*args)


def shape(dims, dtype):
    return jax.ShapeDtypeStruct(dims, dtype)


def mm(a, b):
    return jnp.dot(a, b, preferred_element_type=F32)


def mm_nt(a, b):
    return lax.dot_general(a, b, (((1,), (1,)), ((), ())), preferred_element_type=F32)


def rows_hot(index, first, count):
    rows = lax.broadcasted_iota(jnp.int32, (count, index.shape[1]), 0) + first
    return (rows == index).astype(BF16)


def steps(total, size):
    return [(i, min(size, total - i)) for i in range(0, total, size)]


def rotate_kernel(piece, rotation, *refs):
    outs, (piece_held, rotation_held, groups, sems) = refs[:-4], refs[-4:]
    copies = (
        pltpu.make_async_copy(rotation, rotation_held, sems.at[0]),
        pltpu.make_async_copy(piece, piece_held, sems.at[1]),
    )
    for copy in copies:
        copy.start()
    for copy in copies:
        copy.wait()
    rotated = lax.dot_general(
        rotation_held[...], piece_held[...], (((0,), (0,)), ((), ())), preferred_element_type=F32
    )
    width = groups.shape[1]
    for group in range(groups.shape[0]):
        groups[group] = rotated[group * width : (group + 1) * width, :].astype(BF16)
    mine = lax.axis_index("band")
    for k, out in enumerate(outs):
        out[...] = groups[mine ^ k]


def columns_hot(index, capacity, hot):
    turned = jnp.broadcast_to(index, (LANES, index.shape[1])).T
    for i, n in steps(capacity, LANES):
        lanes = lax.broadcasted_iota(jnp.int32, (turned.shape[0], n), 1) + i
        hot[:, i : i + n] = (turned[:, :n] == lanes).astype(BF16)


def couple_kernel(capacity, weight, node_row, send_row, stiffness, to_ghost, to_own, scatter, spread, local):
    nodes = stiffness.shape[0]
    ghosts = to_own.shape[0]
    slots = to_ghost.shape[2]
    for i, n in steps(node_row.shape[1], nodes):
        picks = rows_hot(node_row[:, i : i + n], capacity, ghosts)
        local[:, i : i + n] = (mm(picks, stiffness[...]) * weight[:, i : i + n]).astype(BF16)
    columns_hot(node_row[...], capacity, scatter)
    for block in range(to_ghost.shape[0]):
        columns_hot(send_row[block : block + 1, :], capacity, spread.at[block])
    for block in range(to_ghost.shape[0]):
        picks = rows_hot(node_row[...], capacity + block * slots, slots)
        to_ghost[block] = mm_nt(local[...], picks).astype(BF16)
    for i, n in steps(capacity, 256):
        to_own[:, i : i + n] = mm(local[...], scatter[:, i : i + n]).astype(BF16)


def pick_rows(send_row, block, values, out):
    picks = rows_hot(send_row[block : block + 1, :], 0, values.shape[1])
    out[...] = mm(values[...], picks).astype(BF16)


def join_kernel(send_row, keep, after, *refs):
    bands = refs[-1].shape[0]
    pieces, (values, near_picked, held) = refs[:bands], refs[bands:]
    mine = lax.axis_index("band")
    for k, piece in enumerate(pieces):
        held[mine ^ k] = piece[...]
    joined = jnp.concatenate([held[p] for p in range(bands)], axis=1)
    values[...] = jnp.where(keep[...] > 0, joined.astype(F32), 0.0).astype(BF16)
    pick_rows(send_row, 0, values, near_picked)


def terms_kernel(send_row, to_own, values, terms, *picked):
    slots = terms.shape[2]
    for block, out in enumerate(picked):
        pick_rows(send_row, block + 1, values, out)
    for block in range(terms.shape[0]):
        terms[block] = mm_nt(values[...], to_own[block * slots : (block + 1) * slots, :])


def cells_kernel(first_step, weight, node_row, stiffness, scatter, potential, values, after, *refs):
    refs = list(refs)
    previous = None if first_step else refs.pop(0)
    out, product, *locals_ = refs
    capacity = values.shape[1]
    nodes = stiffness.shape[0]
    parts = steps(product.shape[1], nodes)
    for (i, n), local in zip(parts, locals_):
        local[...] = mm(values[...], rows_hot(node_row[:, i : i + n], 0, capacity)).astype(BF16)
    for (i, n), local in zip(parts, locals_):
        product[:, i : i + n] = (mm(local[...], stiffness[...]) * weight[:, i : i + n]).astype(BF16)
    for i, n in steps(capacity, 256):
        at = slice(i, i + n)
        sums = mm(product[...], scatter[:, at])
        shifted = sums + (potential[:, at] - CENTER) * values[:, at].astype(F32)
        result = shifted * scale_of(first_step)
        out[:, at] = result if first_step else result - previous[:, at].astype(F32)


def ghost_sum(block, terms, to_ghost, arrived):
    slots = terms.shape[2]
    total = terms[block]
    for other, values in arrived:
        total = total + mm(values, to_ghost[block, other * slots : (other + 1) * slots, :])
    return total.astype(BF16)


def ghost_kernel(terms, to_ghost, *refs):
    blocks = terms.shape[0]
    arrived = [(other, refs[other][...]) for other in range(blocks)]
    for block in range(blocks):
        refs[blocks + block][...] = ghost_sum(block, terms, to_ghost, arrived)


def coupling_rows(slots):
    return round_up(-(-slots // 2), 16)


def parcel_kernel(terms, to_ghost, near_ghosts, far_picked, parcel):
    width, slots = far_picked.shape
    sums = ghost_sum(1, terms, to_ghost, [(0, near_ghosts[...])])
    parcel[:width, :] = jnp.concatenate([far_picked[...], sums], axis=1)
    if parcel.shape[0] > width:
        half = coupling_rows(slots)
        first = parcel.shape[0] - half
        parcel[width:, :] = jnp.zeros((parcel.shape[0] - width, 2 * slots), BF16)
        parcel[first:, :slots] = to_ghost[1, slots : slots + half, :]
        parcel[first : first + slots - half, slots:] = to_ghost[1, slots + half : 2 * slots, :]


def near_kernel(terms, to_ghost, near_ghosts, parcel, after, out):
    width, slots = out.shape
    arrived = [(0, near_ghosts[...]), (1, parcel[:width, :slots])]
    out[...] = ghost_sum(0, terms, to_ghost, arrived)


def scale_of(first_step):
    return (1.0 if first_step else 2.0) / HALF_WIDTH


def own_kernel(first_step, to_own, head, *refs):
    arrived, out = refs[:-1], refs[-1]
    ghosts = jnp.concatenate([ghost[...] for ghost in arrived], axis=1)
    for i, n in steps(out.shape[1], 256):
        at = slice(i, i + n)
        out[:, at] = head[:, at] + mm(ghosts, to_own[:, at]) * scale_of(first_step)


def paired_own_kernel(
    first_step, to_own, head, spread, near_ghosts, far_picked, parcel, first_parcel, out
):
    width, slots = far_picked.shape
    ghosts = jnp.concatenate([near_ghosts[...], parcel[:width, :slots]], axis=1)
    half = coupling_rows(slots)
    start = first_parcel.shape[0] - half
    coupling = jnp.concatenate(
        [first_parcel[start:, :slots], first_parcel[start : start + slots - half, slots:]], axis=0
    )
    returned = parcel[:width, slots:].astype(F32) + mm(far_picked[...], coupling)
    returned = returned.astype(BF16)
    for i, n in steps(out.shape[1], 256):
        at = slice(i, i + n)
        sums = mm(ghosts, to_own[:, at]) + mm(returned, spread[1, :, at])
        out[:, at] = head[:, at] + sums * scale_of(first_step)


def updated_columns(first_step, spread, i, n, total, arrived):
    sums = 0.0
    for block, ghost in enumerate(arrived):
        sums = sums + mm(ghost[...], spread[block, :, i : i + n])
    return (total[:, i : i + n] + sums * scale_of(first_step)).astype(BF16)


def update_kernel(blocks, first_step, spread, send_row, total, *refs):
    arrived, (out, near_picked) = refs[:blocks], refs[blocks:]
    for i, n in steps(out.shape[1], 256):
        out[:, i : i + n] = updated_columns(first_step, spread, i, n, total, arrived)
    near_picked[...] = mm_nt(out[...], spread[0]).astype(BF16)


def last_kernel(blocks, first_step, spread, total, *refs):
    arrived, (out, held, sems) = refs[:blocks], refs[blocks:]
    copies = []
    for part, (i, n) in enumerate(steps(out.shape[1], 256)):
        held[:, i : i + n] = updated_columns(first_step, spread, i, n, total, arrived)
        at = pl.ds(i, n)
        copies.append(pltpu.make_async_copy(held.at[:, at], out.at[:, at], sems.at[part]))
        copies[-1].start()
    for copy in copies:
        copy.wait()


def shards(
    orbitals, rotation, cell_stiffness, cell_scale, potential, cell_nodes, send_rows, domain_rows
):
    domains = lax.axis_size("dom")
    bands = lax.axis_size("band")
    domain = lax.axis_index("dom")
    row_piece = orbitals[0]
    piece_rows, columns = row_piece.shape
    own_rows = domain_rows[0]
    width = columns // bands
    piece_shapes = (shape((width, piece_rows), BF16),) * bands
    pieces = list(call(
        rotate_kernel,
        piece_shapes,
        (row_piece.T, rotation),
        2 * piece_rows * columns * columns,
        scratch=[
            pltpu.VMEM((columns, piece_rows), BF16),
            pltpu.VMEM((columns, columns), BF16),
            pltpu.VMEM((bands, width, piece_rows), BF16),
            pltpu.SemaphoreType.DMA((2,)),
        ],
        in_specs=[ANY, ANY],
        vmem=ROTATE_VMEM,
    ))
    for k in reversed(range(1, bands)):
        pieces[k] = lax.ppermute(pieces[k], "band", [(i, i ^ k) for i in range(bands)])

    capacity = potential.shape[1]
    cells, nodes = cell_nodes.shape[1:]
    slots = send_rows.shape[2]
    nodes_pad = round_up(nodes, 256)
    slots_pad = round_up(slots, 16)
    far = far_groups(domains)
    blocks = 2 + len(far)
    ghosts = blocks * slots_pad
    even = domain % 2 == 0
    send_lists = [
        jnp.where(even, send_rows[0, 3], send_rows[0, 0]),
        jnp.where(even, send_rows[0, 0], send_rows[0, 3]),
    ] + [send_rows[0, g] for g in far]
    send_row = jnp.pad(
        jnp.stack(send_lists), ((0, 0), (0, slots_pad - slots)), constant_values=capacity
    )
    group = (cell_nodes[0] - capacity) // slots
    slot = (cell_nodes[0] - capacity) % slots
    block = jnp.where((group == 0) == even, 0, 1)
    for pos, g in enumerate(far):
        block = jnp.where(group == g, 2 + pos, block)
    ghost_index = capacity + block * slots_pad + slot
    node_list = jnp.where(cell_nodes[0] < capacity, cell_nodes[0], ghost_index)
    node_list = jnp.pad(
        node_list, ((0, 0), (0, nodes_pad - nodes)), constant_values=capacity + ghosts
    ).reshape(-1)
    node_row = node_list[None, :]
    stiffness = jnp.pad(cell_stiffness, ((0, nodes_pad - nodes), (0, nodes_pad - nodes)))

    cell_total = (own_rows - FACE_NODES) // (DEGREE * FACE_NODES)
    cell_live = jnp.arange(cell_scale.shape[1], dtype=jnp.int32) < cell_total
    weight = jnp.where(cell_live, cell_scale[0], jnp.zeros_like(cell_scale[0]))
    weight = jnp.repeat(weight, nodes_pad)[None, :]

    local_rows = cells * nodes_pad
    cell_flops = 2 * local_rows * nodes_pad
    to_ghost, to_own, scatter, spread = call(
        functools.partial(couple_kernel, capacity),
        (
            shape((blocks, ghosts, slots_pad), BF16),
            shape((ghosts, capacity), BF16),
            shape((local_rows, capacity), BF16),
            shape((blocks, slots_pad, capacity), BF16),
        ),
        (weight, node_row, send_row, stiffness),
        (cell_flops + 2 * local_rows * (ghosts + capacity)) * ghosts,
        scratch=[pltpu.VMEM((ghosts, local_rows), BF16)],
    )
    block_shape = shape((width, slots_pad), BF16)
    keep = (jnp.arange(capacity, dtype=jnp.int32) < own_rows).astype(jnp.int32)[None, :]
    current, near_picked = call(
        join_kernel,
        (shape((width, capacity), BF16), block_shape),
        (send_row, keep, to_ghost, *pieces),
        2 * slots_pad * capacity * width,
        scratch=[pltpu.VMEM((bands, width, piece_rows), BF16)],
        in_specs=[VMEM, VMEM, ANY] + [VMEM] * bands,
    )
    previous = None
    parcel_rows = round_up(width, 16) + coupling_rows(slots_pad)
    first_parcel = None
    for filter_step in range(FILTER_STEPS):
        first, last = filter_step == 0, filter_step == FILTER_STEPS - 1
        near = swap(near_picked, 0)
        terms, *picked = call(
            terms_kernel,
            (shape((blocks, width, slots_pad), F32),) + (block_shape,) * (blocks - 1),
            (send_row, to_own, current),
            4 * ghosts * capacity * width,
        )
        if far:
            arrived = [near, *exchange(picked, False)]
            ready = terms
        else:
            parcel = call(
                parcel_kernel,
                shape((parcel_rows if first else width, 2 * slots_pad), BF16),
                (terms, to_ghost, near, picked[0]),
                2 * slots_pad * slots_pad * width,
            )
            ready = parcel
            parcel = swap(parcel, 1)
            first_parcel = parcel if first else first_parcel
        history = () if first else (previous,)
        head = call(
            functools.partial(cells_kernel, first),
            shape((width, capacity), F32),
            (weight, node_row, stiffness, scatter, potential, current, ready, *history),
            (cell_flops + 4 * local_rows * capacity) * width,
            scratch=[pltpu.VMEM((width, local_rows), BF16)] + [pltpu.VMEM((width, nodes_pad), BF16)] * cells,
            in_specs=[VMEM] * 6 + [ANY] + [VMEM] * len(history),
        )
        own_flops = 2 * capacity * ghosts * width
        if far:
            sums = call(
                ghost_kernel,
                (block_shape,) * blocks,
                (terms, to_ghost, *arrived),
                2 * ghosts * ghosts * width,
            )
            returned = [swap(sums[0], 0), *exchange(sums[1:], True)]
            total = call(
                functools.partial(own_kernel, first),
                shape((width, capacity), F32),
                (to_own, head, *arrived),
                own_flops,
            )
        else:
            sums = call(
                near_kernel,
                block_shape,
                (terms, to_ghost, near, parcel, head),
                2 * ghosts * slots_pad * width,
                in_specs=[VMEM] * 4 + [ANY],
            )
            returned = [swap(sums, 0)]
            total = call(
                functools.partial(paired_own_kernel, first),
                shape((width, capacity), F32),
                (to_own, head, spread, near, picked[0], parcel, first_parcel),
                own_flops,
            )
        update_flops = 2 * capacity * (ghosts + slots_pad * len(returned)) * width
        if last:
            current = call(
                functools.partial(last_kernel, len(returned), first),
                shape((width, capacity), BF16),
                (spread, total, *returned),
                update_flops,
                scratch=[
                    pltpu.VMEM((width, capacity), BF16),
                    pltpu.SemaphoreType.DMA((len(steps(capacity, 256)),)),
                ],
                out_specs=ANY,
            )
        else:
            following, near_picked = call(
                functools.partial(update_kernel, len(returned), first),
                (shape((width, capacity), BF16), block_shape),
                (spread, send_row, total, *returned),
                update_flops,
            )
            previous, current = current, following
    return current.T[None]


def solution(mesh):
    return jax.shard_map(
        shards,
        mesh=mesh,
        in_specs=(
            P("dom", "band", None),
            P(),
            P(),
            P("dom", None),
            P("dom", None),
            P("dom", None, None),
            P("dom", None, None),
            P("dom"),
        ),
        out_specs=P("dom", None, "band"),
        check_vma=False,
    )
```

```python
import functools

import jax
import jax.numpy as jnp
from jax import lax
from jax.experimental import pallas as pl
from jax.experimental.pallas import tpu as pltpu
from jax.sharding import PartitionSpec as P

DEGREE = 8
FILTER_STEPS = 3
FACE_NODES = 81

OFFSETS = (1, 8, -8, -1)
CENTER = 5.0
HALF_WIDTH = 5.0
BF16 = jnp.bfloat16
F32 = jnp.float32
VMEM = pl.BlockSpec(memory_space=pltpu.VMEM)
ANY = pl.BlockSpec(memory_space=pl.ANY)
LANES = 128
DIGIT = 64
DIGIT_ROWS = 16
ROTATE_VMEM = 56 << 20


def round_up(value, multiple):
    return -(-value // multiple) * multiple


def swap(value, first):
    domains = lax.axis_size("dom")
    pairs = []
    for low in range(first, domains - 1, 2):
        pairs += [(low, low + 1), (low + 1, low)]
    return lax.ppermute(value, "dom", pairs)


def shift(value, by):
    domains = lax.axis_size("dom")
    pairs = [(i, i + by) for i in range(domains) if 0 <= i + by < domains]
    return lax.ppermute(value, "dom", pairs)


def far_groups(domains):
    return [g for g, offset in enumerate(OFFSETS) if abs(offset) > 1 and abs(offset) < domains]


def exchange(blocks, to_owner):
    out = [swap(blocks[0], 1)]
    for block, group in zip(blocks[1:], far_groups(lax.axis_size("dom"))):
        out.append(shift(block, OFFSETS[group] if to_owner else -OFFSETS[group]))
    return out


def call(kernel, out_shape, args, flops, scratch=(), in_specs=None, out_specs=None, vmem=16 << 20):
    outs = out_shape if isinstance(out_shape, (tuple, list)) else (out_shape,)
    size = sum(a.size * a.dtype.itemsize for a in list(args) + list(outs))
    return pl.pallas_call(
        kernel,
        out_shape=out_shape,
        in_specs=in_specs or [VMEM] * len(args),
        out_specs=out_specs or jax.tree.map(lambda _: VMEM, out_shape),
        scratch_shapes=list(scratch),
        cost_estimate=pl.CostEstimate(flops=flops, bytes_accessed=size, transcendentals=0),
        compiler_params=pltpu.CompilerParams(vmem_limit_bytes=vmem),
    )(*args)


def shape(dims, dtype):
    return jax.ShapeDtypeStruct(dims, dtype)


def mm(a, b):
    return jnp.dot(a, b, preferred_element_type=F32)


def mm_nt(a, b):
    return lax.dot_general(a, b, (((1,), (1,)), ((), ())), preferred_element_type=F32)


def rows_hot(index, first, count):
    rows = lax.broadcasted_iota(jnp.int32, (count, index.shape[1]), 0) + first
    return (rows == index).astype(BF16)


def steps(total, size):
    return [(i, min(size, total - i)) for i in range(0, total, size)]


def rotate_kernel(piece, rotation, *refs):
    outs, (piece_held, rotation_held, groups, sems) = refs[:-4], refs[-4:]
    copies = (
        pltpu.make_async_copy(rotation, rotation_held, sems.at[0]),
        pltpu.make_async_copy(piece, piece_held, sems.at[1]),
    )
    for copy in copies:
        copy.start()
    for copy in copies:
        copy.wait()
    rotated = lax.dot_general(
        rotation_held[...], piece_held[...], (((0,), (0,)), ((), ())), preferred_element_type=F32
    )
    width = groups.shape[1]
    for group in range(groups.shape[0]):
        groups[group] = rotated[group * width : (group + 1) * width, :].astype(BF16)
    mine = lax.axis_index("band")
    for k, out in enumerate(outs):
        out[...] = groups[mine ^ k]


def columns_hot(index, capacity, hot):
    turned = jnp.broadcast_to(index, (LANES, index.shape[1])).T
    for i, n in steps(capacity, LANES):
        lanes = lax.broadcasted_iota(jnp.int32, (turned.shape[0], n), 1) + i
        hot[:, i : i + n] = (turned[:, :n] == lanes).astype(BF16)


def couple_kernel(capacity, weight, node_row, send_row, stiffness, to_ghost, to_own, scatter, spread, to_near, far_near, local):
    nodes = stiffness.shape[0]
    ghosts = to_own.shape[0]
    slots = to_ghost.shape[2]
    for i, n in steps(node_row.shape[1], nodes):
        picks = rows_hot(node_row[:, i : i + n], capacity, ghosts)
        local[:, i : i + n] = (mm(picks, stiffness[...]) * weight[:, i : i + n]).astype(BF16)
    columns_hot(node_row[...], capacity, scatter)
    for block in range(to_ghost.shape[0]):
        columns_hot(send_row[block : block + 1, :], capacity, spread.at[block])
    for block in range(to_ghost.shape[0]):
        picks = rows_hot(node_row[...], capacity + block * slots, slots)
        to_ghost[block] = mm_nt(local[...], picks).astype(BF16)
    for i, n in steps(capacity, 256):
        to_own[:, i : i + n] = mm(local[...], scatter[:, i : i + n]).astype(BF16)
    to_near[...] = mm_nt(to_own[...], spread[0]).astype(BF16)
    far_near[...] = mm_nt(spread[1], spread[0]).astype(BF16)


def same_kernel(capacity, first_near, same):
    slots = same.shape[0]
    digits = first_near[first_near.shape[0] - DIGIT_ROWS :, :].astype(F32)
    rows = digits[0:1, :] * DIGIT + digits[1:2, :]
    turned = jnp.broadcast_to(rows, (slots, slots)).T
    same[...] = ((turned == rows) & (turned < capacity)).astype(BF16)


def pick_rows(send_row, block, values, out):
    picks = rows_hot(send_row[block : block + 1, :], 0, values.shape[1])
    out[: values.shape[0], :] = mm(values[...], picks).astype(BF16)


def join_kernel(send_row, keep, digits, after, *refs):
    bands = refs[-1].shape[0]
    pieces, (values, near_picked, held) = refs[:bands], refs[bands:]
    mine = lax.axis_index("band")
    for k, piece in enumerate(pieces):
        held[mine ^ k] = piece[...]
    joined = jnp.concatenate([held[p] for p in range(bands)], axis=1)
    values[...] = jnp.where(keep[...] > 0, joined.astype(F32), 0.0).astype(BF16)
    if near_picked.shape[0] > values.shape[0]:
        near_picked[...] = jnp.zeros(near_picked.shape, BF16)
        near_picked[near_picked.shape[0] - DIGIT_ROWS :, :] = digits[...]
    pick_rows(send_row, 0, values, near_picked)


def terms_kernel(send_row, to_own, values, terms, *picked):
    slots = terms.shape[2]
    for block, out in enumerate(picked):
        pick_rows(send_row, block + 1, values, out)
    for block in range(terms.shape[0]):
        terms[block] = mm_nt(values[...], to_own[block * slots : (block + 1) * slots, :])


def cells_kernel(first_step, near_wanted, weight, node_row, stiffness, scatter, spread, potential, values, after, *refs):
    refs = list(refs)
    previous = None if first_step else refs.pop(0)
    out = refs.pop(0)
    near_out = refs.pop(0) if near_wanted else None
    product, *locals_ = refs
    capacity = values.shape[1]
    nodes = stiffness.shape[0]
    parts = steps(product.shape[1], nodes)
    for (i, n), local in zip(parts, locals_):
        local[...] = mm(values[...], rows_hot(node_row[:, i : i + n], 0, capacity)).astype(BF16)
    for (i, n), local in zip(parts, locals_):
        product[:, i : i + n] = (mm(local[...], stiffness[...]) * weight[:, i : i + n]).astype(BF16)
    for i, n in steps(capacity, 256):
        at = slice(i, i + n)
        sums = mm(product[...], scatter[:, at])
        shifted = sums + (potential[:, at] - CENTER) * values[:, at].astype(F32)
        result = shifted * scale_of(first_step)
        out[:, at] = result if first_step else result - previous[:, at].astype(F32)
    if near_wanted:
        near_out[...] = mm_nt(out[...].astype(BF16), spread[0])


def ghost_sum(block, terms, to_ghost, arrived):
    slots = terms.shape[2]
    total = terms[block]
    for other, values in arrived:
        total = total + mm(values, to_ghost[block, other * slots : (other + 1) * slots, :])
    return total.astype(BF16)


def ghost_kernel(terms, to_ghost, *refs):
    blocks = terms.shape[0]
    arrived = [(other, refs[other][...]) for other in range(blocks)]
    for block in range(blocks):
        refs[blocks + block][...] = ghost_sum(block, terms, to_ghost, arrived)


def coupling_rows(slots):
    return round_up(-(-slots // 2), 16)


def parcel_kernel(terms, to_ghost, near_ghosts, far_picked, parcel):
    width, slots = far_picked.shape
    sums = ghost_sum(1, terms, to_ghost, [(0, near_ghosts[:width, :])])
    if parcel.shape[0] > width:
        half = coupling_rows(slots)
        first = parcel.shape[0] - half
        parcel[...] = jnp.zeros(parcel.shape, BF16)
        parcel[first:, :slots] = to_ghost[1, slots : slots + half, :]
        parcel[first : first + slots - half, slots:] = to_ghost[1, slots + half : 2 * slots, :]
    parcel[:width, :] = jnp.concatenate([far_picked[...], sums], axis=1)


def returned_sums(far_picked, parcel, first_parcel):
    width, slots = far_picked.shape
    half = coupling_rows(slots)
    start = first_parcel.shape[0] - half
    coupling = jnp.concatenate(
        [first_parcel[start:, :slots], first_parcel[start : start + slots - half, slots:]], axis=0
    )
    returned = parcel[:width, slots:].astype(F32) + mm(far_picked[...], coupling)
    return returned.astype(BF16)


def pair_kernel(
    first_step, terms, to_ghost, near_ghosts, far_picked, parcel, first_parcel, near_head, to_near, far_near, out
):
    width, slots = far_picked.shape
    far_ghosts = parcel[:width, :slots]
    sums = ghost_sum(0, terms, to_ghost, [(0, near_ghosts[:width, :]), (1, far_ghosts)])
    returned = returned_sums(far_picked, parcel, first_parcel)
    known = mm(near_ghosts[:width, :], to_near[:slots, :]) + mm(far_ghosts, to_near[slots:, :])
    known = near_head[...] + (known + mm(returned, far_near[...])) * scale_of(first_step)
    out[...] = jnp.concatenate([sums, known.astype(BF16)], axis=1)


def advance_kernel(
    first_step, spread, same, send_row, to_own, to_ghost, total, sent, arrived, values, near_ghosts, far_picked, terms, parcel
):
    slots = far_picked.shape[1]
    sums = arrived[:, :slots]
    for i, n in steps(values.shape[1], 256):
        added = mm(sums, spread[0, :, i : i + n]) * scale_of(first_step)
        values[:, i : i + n] = (total[:, i : i + n] + added).astype(BF16)
    near = mm(sent[:, :slots], same[...]) * scale_of(first_step) + arrived[:, slots:].astype(F32)
    near_ghosts[...] = near.astype(BF16)
    terms_kernel(send_row, to_own, values, terms, far_picked)
    parcel_kernel(terms, to_ghost, near_ghosts, far_picked, parcel)


def near_kernel(terms, to_ghost, near_ghosts, parcel, after, out):
    width, slots = out.shape
    arrived = [(0, near_ghosts[:width, :]), (1, parcel[:width, :slots])]
    out[...] = ghost_sum(0, terms, to_ghost, arrived)


def scale_of(first_step):
    return (1.0 if first_step else 2.0) / HALF_WIDTH


def own_kernel(first_step, to_own, head, *refs):
    arrived, out = refs[:-1], refs[-1]
    ghosts = jnp.concatenate([ghost[...] for ghost in arrived], axis=1)
    for i, n in steps(out.shape[1], 256):
        at = slice(i, i + n)
        out[:, at] = head[:, at] + mm(ghosts, to_own[:, at]) * scale_of(first_step)


def paired_own_kernel(
    first_step, to_own, head, spread, near_ghosts, far_picked, parcel, first_parcel, out
):
    width, slots = far_picked.shape
    ghosts = jnp.concatenate([near_ghosts[:width, :], parcel[:width, :slots]], axis=1)
    returned = returned_sums(far_picked, parcel, first_parcel)
    for i, n in steps(out.shape[1], 256):
        at = slice(i, i + n)
        sums = mm(ghosts, to_own[:, at]) + mm(returned, spread[1, :, at])
        out[:, at] = head[:, at] + sums * scale_of(first_step)


def updated_columns(first_step, spread, i, n, total, arrived):
    sums = 0.0
    for block, ghost in enumerate(arrived):
        sums = sums + mm(ghost[...], spread[block, :, i : i + n])
    return (total[:, i : i + n] + sums * scale_of(first_step)).astype(BF16)


def update_kernel(blocks, first_step, spread, send_row, total, *refs):
    arrived, (out, near_picked) = refs[:blocks], refs[blocks:]
    for i, n in steps(out.shape[1], 256):
        out[:, i : i + n] = updated_columns(first_step, spread, i, n, total, arrived)
    near_picked[...] = mm_nt(out[...], spread[0]).astype(BF16)


def last_kernel(blocks, first_step, spread, total, *refs):
    arrived, (out, held, sems) = refs[:blocks], refs[blocks:]
    copies = []
    for part, (i, n) in enumerate(steps(out.shape[1], 256)):
        held[:, i : i + n] = updated_columns(first_step, spread, i, n, total, arrived)
        at = pl.ds(i, n)
        copies.append(pltpu.make_async_copy(held.at[:, at], out.at[:, at], sems.at[part]))
        copies[-1].start()
    for copy in copies:
        copy.wait()


def shards(
    orbitals, rotation, cell_stiffness, cell_scale, potential, cell_nodes, send_rows, domain_rows
):
    domains = lax.axis_size("dom")
    bands = lax.axis_size("band")
    domain = lax.axis_index("dom")
    row_piece = orbitals[0]
    piece_rows, columns = row_piece.shape
    own_rows = domain_rows[0]
    width = columns // bands
    piece_shapes = (shape((width, piece_rows), BF16),) * bands
    pieces = list(call(
        rotate_kernel,
        piece_shapes,
        (row_piece.T, rotation),
        2 * piece_rows * columns * columns,
        scratch=[
            pltpu.VMEM((columns, piece_rows), BF16),
            pltpu.VMEM((columns, columns), BF16),
            pltpu.VMEM((bands, width, piece_rows), BF16),
            pltpu.SemaphoreType.DMA((2,)),
        ],
        in_specs=[ANY, ANY],
        vmem=ROTATE_VMEM,
    ))
    for k in reversed(range(1, bands)):
        pieces[k] = lax.ppermute(pieces[k], "band", [(i, i ^ k) for i in range(bands)])

    capacity = potential.shape[1]
    cells, nodes = cell_nodes.shape[1:]
    slots = send_rows.shape[2]
    nodes_pad = round_up(nodes, 256)
    slots_pad = round_up(slots, 16)
    far = far_groups(domains)
    blocks = 2 + len(far)
    ghosts = blocks * slots_pad
    even = domain % 2 == 0
    send_lists = [
        jnp.where(even, send_rows[0, 3], send_rows[0, 0]),
        jnp.where(even, send_rows[0, 0], send_rows[0, 3]),
    ] + [send_rows[0, g] for g in far]
    send_row = jnp.pad(
        jnp.stack(send_lists), ((0, 0), (0, slots_pad - slots)), constant_values=capacity
    )
    group = (cell_nodes[0] - capacity) // slots
    slot = (cell_nodes[0] - capacity) % slots
    block = jnp.where((group == 0) == even, 0, 1)
    for pos, g in enumerate(far):
        block = jnp.where(group == g, 2 + pos, block)
    ghost_index = capacity + block * slots_pad + slot
    node_list = jnp.where(cell_nodes[0] < capacity, cell_nodes[0], ghost_index)
    node_list = jnp.pad(
        node_list, ((0, 0), (0, nodes_pad - nodes)), constant_values=capacity + ghosts
    ).reshape(-1)
    node_row = node_list[None, :]
    stiffness = jnp.pad(cell_stiffness, ((0, nodes_pad - nodes), (0, nodes_pad - nodes)))

    cell_total = (own_rows - FACE_NODES) // (DEGREE * FACE_NODES)
    cell_live = jnp.arange(cell_scale.shape[1], dtype=jnp.int32) < cell_total
    weight = jnp.where(cell_live, cell_scale[0], jnp.zeros_like(cell_scale[0]))
    weight = jnp.repeat(weight, nodes_pad)[None, :]

    local_rows = cells * nodes_pad
    cell_flops = 2 * local_rows * nodes_pad
    to_ghost, to_own, scatter, spread, to_near, far_near = call(
        functools.partial(couple_kernel, capacity),
        (
            shape((blocks, ghosts, slots_pad), BF16),
            shape((ghosts, capacity), BF16),
            shape((local_rows, capacity), BF16),
            shape((blocks, slots_pad, capacity), BF16),
            shape((ghosts, slots_pad), BF16),
            shape((slots_pad, slots_pad), BF16),
        ),
        (weight, node_row, send_row, stiffness),
        (cell_flops + 2 * local_rows * (ghosts + capacity)) * ghosts,
        scratch=[pltpu.VMEM((ghosts, local_rows), BF16)],
    )
    block_shape = shape((width, slots_pad), BF16)
    keep = (jnp.arange(capacity, dtype=jnp.int32) < own_rows).astype(jnp.int32)[None, :]
    near_rows = width if far else round_up(width, 16) + DIGIT_ROWS
    digits = jnp.pad(
        jnp.stack([send_row[0] // DIGIT, send_row[0] % DIGIT]), ((0, DIGIT_ROWS - 2), (0, 0))
    ).astype(BF16)
    current, near_picked = call(
        join_kernel,
        (shape((width, capacity), BF16), shape((near_rows, slots_pad), BF16)),
        (send_row, keep, digits, to_ghost, *pieces),
        2 * slots_pad * capacity * width,
        scratch=[pltpu.VMEM((bands, width, piece_rows), BF16)],
        in_specs=[VMEM, VMEM, VMEM, ANY] + [VMEM] * bands,
    )
    previous = None
    parcel_rows = round_up(width, 16) + coupling_rows(slots_pad)
    terms_shape = shape((blocks, width, slots_pad), F32)
    terms_flops = 4 * ghosts * capacity * width
    for filter_step in range(FILTER_STEPS):
        first, last = filter_step == 0, filter_step == FILTER_STEPS - 1
        if first or far:
            near = swap(near_picked, 0)
            terms, *picked = call(
                terms_kernel,
                (terms_shape,) + (block_shape,) * (blocks - 1),
                (send_row, to_own, current),
                terms_flops,
            )
        if far:
            arrived = [near, *exchange(picked, False)]
            ready = terms
        else:
            if first:
                same = call(
                    functools.partial(same_kernel, capacity),
                    shape((slots_pad, slots_pad), BF16),
                    (near,),
                    slots_pad * slots_pad,
                )
                ready = call(
                    parcel_kernel,
                    shape((parcel_rows, 2 * slots_pad), BF16),
                    (terms, to_ghost, near, picked[0]),
                    2 * slots_pad * slots_pad * width,
                )
            parcel = swap(ready, 1)
            first_parcel = parcel if first else first_parcel
        history = () if first else (previous,)
        near_wanted = not far and not last
        head, *near_head = call(
            functools.partial(cells_kernel, first, near_wanted),
            (shape((width, capacity), F32),) + (shape((width, slots_pad), F32),) * near_wanted,
            (weight, node_row, stiffness, scatter, spread, potential, current, ready, *history),
            (cell_flops + 4 * local_rows * capacity) * width,
            scratch=[pltpu.VMEM((width, local_rows), BF16)] + [pltpu.VMEM((width, nodes_pad), BF16)] * cells,
            in_specs=[VMEM] * 7 + [ANY] + [VMEM] * len(history),
        )
        own_flops = 2 * capacity * ghosts * width
        if far:
            sums = call(
                ghost_kernel,
                (block_shape,) * blocks,
                (terms, to_ghost, *arrived),
                2 * ghosts * ghosts * width,
            )
            returned = [swap(sums[0], 0), *exchange(sums[1:], True)]
            total = call(
                functools.partial(own_kernel, first),
                shape((width, capacity), F32),
                (to_own, head, *arrived),
                own_flops,
            )
        else:
            if last:
                sent = call(
                    near_kernel,
                    block_shape,
                    (terms, to_ghost, near, parcel, head),
                    2 * ghosts * slots_pad * width,
                    in_specs=[VMEM] * 4 + [ANY],
                )
            else:
                sent = call(
                    functools.partial(pair_kernel, first),
                    shape((width, 2 * slots_pad), BF16),
                    (terms, to_ghost, near, picked[0], parcel, first_parcel, *near_head, to_near, far_near),
                    6 * ghosts * slots_pad * width,
                )
            returned = [swap(sent, 0)]
            total = call(
                functools.partial(paired_own_kernel, first),
                shape((width, capacity), F32),
                (to_own, head, spread, near, picked[0], parcel, first_parcel),
                own_flops,
            )
        update_flops = 2 * capacity * (ghosts + slots_pad * len(returned)) * width
        if last:
            current = call(
                functools.partial(last_kernel, len(returned), first),
                shape((width, capacity), BF16),
                (spread, total, *returned),
                update_flops,
                scratch=[
                    pltpu.VMEM((width, capacity), BF16),
                    pltpu.SemaphoreType.DMA((len(steps(capacity, 256)),)),
                ],
                out_specs=ANY,
            )
        elif not far:
            following, near, far_picked, terms, ready = call(
                functools.partial(advance_kernel, first),
                (
                    shape((width, capacity), BF16),
                    block_shape,
                    block_shape,
                    terms_shape,
                    shape((width, 2 * slots_pad), BF16),
                ),
                (spread, same, send_row, to_own, to_ghost, total, sent, *returned),
                update_flops + terms_flops,
            )
            picked = [far_picked]
            previous, current = current, following
        else:
            following, near_picked = call(
                functools.partial(update_kernel, len(returned), first),
                (shape((width, capacity), BF16), block_shape),
                (spread, send_row, total, *returned),
                update_flops,
            )
            previous, current = current, following
    return current.T[None]


def solution(mesh):
    return jax.shard_map(
        shards,
        mesh=mesh,
        in_specs=(
            P("dom", "band", None),
            P(),
            P(),
            P("dom", None),
            P("dom", None),
            P("dom", None, None),
            P("dom", None, None),
            P("dom"),
        ),
        out_specs=P("dom", None, "band"),
        check_vma=False,
    )
```

```python
import functools

import jax
import jax.numpy as jnp
from jax import lax
from jax.experimental import pallas as pl
from jax.experimental.pallas import tpu as pltpu
from jax.sharding import PartitionSpec as P

DEGREE = 8
FILTER_STEPS = 3
FACE_NODES = 81

OFFSETS = (1, 8, -8, -1)
CENTER = 5.0
HALF_WIDTH = 5.0
BF16 = jnp.bfloat16
F32 = jnp.float32
VMEM = pl.BlockSpec(memory_space=pltpu.VMEM)
ANY = pl.BlockSpec(memory_space=pl.ANY)
LANES = 128
DIGIT = 64
DIGIT_ROWS = 16
ROTATE_VMEM = 53 << 20


def round_up(value, multiple):
    return -(-value // multiple) * multiple


def swap(value, first):
    domains = lax.axis_size("dom")
    pairs = []
    for low in range(first, domains - 1, 2):
        pairs += [(low, low + 1), (low + 1, low)]
    return lax.ppermute(value, "dom", pairs)


def shift(value, by):
    domains = lax.axis_size("dom")
    pairs = [(i, i + by) for i in range(domains) if 0 <= i + by < domains]
    return lax.ppermute(value, "dom", pairs)


def far_groups(domains):
    return [g for g, offset in enumerate(OFFSETS) if abs(offset) > 1 and abs(offset) < domains]


def exchange(blocks, to_owner):
    out = [swap(blocks[0], 1)]
    for block, group in zip(blocks[1:], far_groups(lax.axis_size("dom"))):
        out.append(shift(block, OFFSETS[group] if to_owner else -OFFSETS[group]))
    return out


def call(kernel, out_shape, args, flops, scratch=(), in_specs=None, out_specs=None, vmem=16 << 20):
    outs = out_shape if isinstance(out_shape, (tuple, list)) else (out_shape,)
    size = sum(a.size * a.dtype.itemsize for a in list(args) + list(outs))
    return pl.pallas_call(
        kernel,
        out_shape=out_shape,
        in_specs=in_specs or [VMEM] * len(args),
        out_specs=out_specs or jax.tree.map(lambda _: VMEM, out_shape),
        scratch_shapes=list(scratch),
        cost_estimate=pl.CostEstimate(flops=flops, bytes_accessed=size, transcendentals=0),
        compiler_params=pltpu.CompilerParams(vmem_limit_bytes=vmem),
    )(*args)


def shape(dims, dtype):
    return jax.ShapeDtypeStruct(dims, dtype)


def mm(a, b):
    return jnp.dot(a, b, preferred_element_type=F32)


def mm_nt(a, b):
    return lax.dot_general(a, b, (((1,), (1,)), ((), ())), preferred_element_type=F32)


def rows_hot(index, first, count):
    rows = lax.broadcasted_iota(jnp.int32, (count, index.shape[1]), 0) + first
    return (rows == index).astype(BF16)


def steps(total, size):
    return [(i, min(size, total - i)) for i in range(0, total, size)]


def rotate_kernel(piece, rotation, *refs):
    outs, (piece_held, rotation_held, groups, sems) = refs[:-4], refs[-4:]
    copies = (
        pltpu.make_async_copy(rotation, rotation_held, sems.at[0]),
        pltpu.make_async_copy(piece, piece_held, sems.at[1]),
    )
    for copy in copies:
        copy.start()
    for copy in copies:
        copy.wait()
    rotated = lax.dot_general(
        rotation_held[...], piece_held[...], (((0,), (0,)), ((), ())), preferred_element_type=F32
    )
    width = groups.shape[1]
    for group in range(groups.shape[0]):
        groups[group] = rotated[group * width : (group + 1) * width, :].astype(BF16)
    mine = lax.axis_index("band")
    for k, out in enumerate(outs):
        out[...] = groups[mine ^ k]


def columns_hot(index, capacity, hot):
    turned = jnp.broadcast_to(index, (LANES, index.shape[1])).T
    for i, n in steps(capacity, LANES):
        lanes = lax.broadcasted_iota(jnp.int32, (turned.shape[0], n), 1) + i
        hot[:, i : i + n] = (turned[:, :n] == lanes).astype(BF16)


def couple_kernel(capacity, weight, node_row, send_row, stiffness, to_ghost, to_own, scatter, spread, to_near, far_near, local):
    nodes = stiffness.shape[0]
    ghosts = to_own.shape[0]
    slots = to_ghost.shape[2]
    for i, n in steps(node_row.shape[1], nodes):
        picks = rows_hot(node_row[:, i : i + n], capacity, ghosts)
        local[:, i : i + n] = (mm(picks, stiffness[...]) * weight[:, i : i + n]).astype(BF16)
    columns_hot(node_row[...], capacity, scatter)
    for block in range(to_ghost.shape[0]):
        columns_hot(send_row[block : block + 1, :], capacity, spread.at[block])
    for block in range(to_ghost.shape[0]):
        picks = rows_hot(node_row[...], capacity + block * slots, slots)
        to_ghost[block] = mm_nt(local[...], picks).astype(BF16)
    for i, n in steps(capacity, 256):
        to_own[:, i : i + n] = mm(local[...], scatter[:, i : i + n]).astype(BF16)
    to_near[...] = mm_nt(to_own[...], spread[0]).astype(BF16)
    far_near[...] = mm_nt(spread[1], spread[0]).astype(BF16)


def same_kernel(capacity, first_near, same):
    slots = same.shape[0]
    digits = first_near[first_near.shape[0] - DIGIT_ROWS :, :].astype(F32)
    rows = digits[0:1, :] * DIGIT + digits[1:2, :]
    turned = jnp.broadcast_to(rows, (slots, slots)).T
    same[...] = ((turned == rows) & (turned < capacity)).astype(BF16)


def pick_rows(send_row, block, values, out):
    picks = rows_hot(send_row[block : block + 1, :], 0, values.shape[1])
    out[: values.shape[0], :] = mm(values[...], picks).astype(BF16)


def join_kernel(send_row, keep, digits, after, *refs):
    bands = refs[-1].shape[0]
    pieces, (values, near_picked, held) = refs[:bands], refs[bands:]
    mine = lax.axis_index("band")
    for k, piece in enumerate(pieces):
        held[mine ^ k] = piece[...]
    joined = jnp.concatenate([held[p] for p in range(bands)], axis=1)
    values[...] = jnp.where(keep[...] > 0, joined.astype(F32), 0.0).astype(BF16)
    if near_picked.shape[0] > values.shape[0]:
        near_picked[...] = jnp.zeros(near_picked.shape, BF16)
        near_picked[near_picked.shape[0] - DIGIT_ROWS :, :] = digits[...]
    pick_rows(send_row, 0, values, near_picked)


def terms_kernel(send_row, to_own, values, terms, *picked):
    slots = terms.shape[2]
    for block, out in enumerate(picked):
        pick_rows(send_row, block + 1, values, out)
    for block in range(terms.shape[0]):
        terms[block] = mm_nt(values[...], to_own[block * slots : (block + 1) * slots, :])


def cells_kernel(first_step, near_wanted, weight, node_row, stiffness, scatter, spread, potential, values, after, *refs):
    refs = list(refs)
    previous = None if first_step else refs.pop(0)
    out = refs.pop(0)
    near_out = refs.pop(0) if near_wanted else None
    product, *locals_ = refs
    capacity = values.shape[1]
    nodes = stiffness.shape[0]
    parts = steps(product.shape[1], nodes)
    for (i, n), local in zip(parts, locals_):
        local[...] = mm(values[...], rows_hot(node_row[:, i : i + n], 0, capacity)).astype(BF16)
    for (i, n), local in zip(parts, locals_):
        product[:, i : i + n] = (mm(local[...], stiffness[...]) * weight[:, i : i + n]).astype(BF16)
    for i, n in steps(capacity, 256):
        at = slice(i, i + n)
        sums = mm(product[...], scatter[:, at])
        shifted = sums + (potential[:, at] - CENTER) * values[:, at].astype(F32)
        result = shifted * scale_of(first_step)
        out[:, at] = result if first_step else result - previous[:, at].astype(F32)
    if near_wanted:
        near_out[...] = mm_nt(out[...].astype(BF16), spread[0])


def ghost_sum(block, terms, to_ghost, arrived):
    slots = terms.shape[2]
    total = terms[block]
    for other, values in arrived:
        total = total + mm(values, to_ghost[block, other * slots : (other + 1) * slots, :])
    return total.astype(BF16)


def ghost_kernel(terms, to_ghost, *refs):
    blocks = terms.shape[0]
    arrived = [(other, refs[other][...]) for other in range(blocks)]
    for block in range(blocks):
        refs[blocks + block][...] = ghost_sum(block, terms, to_ghost, arrived)


def coupling_rows(slots):
    return round_up(-(-slots // 2), 16)


def parcel_kernel(terms, to_ghost, near_ghosts, far_picked, parcel):
    width, slots = far_picked.shape
    sums = ghost_sum(1, terms, to_ghost, [(0, near_ghosts[:width, :])])
    if parcel.shape[0] > width:
        half = coupling_rows(slots)
        first = parcel.shape[0] - half
        parcel[...] = jnp.zeros(parcel.shape, BF16)
        parcel[first:, :slots] = to_ghost[1, slots : slots + half, :]
        parcel[first : first + slots - half, slots:] = to_ghost[1, slots + half : 2 * slots, :]
    parcel[:width, :] = jnp.concatenate([far_picked[...], sums], axis=1)


def returned_sums(far_picked, parcel, first_parcel):
    width, slots = far_picked.shape
    half = coupling_rows(slots)
    start = first_parcel.shape[0] - half
    coupling = jnp.concatenate(
        [first_parcel[start:, :slots], first_parcel[start : start + slots - half, slots:]], axis=0
    )
    returned = parcel[:width, slots:].astype(F32) + mm(far_picked[...], coupling)
    return returned.astype(BF16)


def pair_kernel(
    first_step, terms, to_ghost, near_ghosts, far_picked, parcel, first_parcel, near_head, to_near, far_near, out
):
    width, slots = far_picked.shape
    far_ghosts = parcel[:width, :slots]
    sums = ghost_sum(0, terms, to_ghost, [(0, near_ghosts[:width, :]), (1, far_ghosts)])
    returned = returned_sums(far_picked, parcel, first_parcel)
    known = mm(near_ghosts[:width, :], to_near[:slots, :]) + mm(far_ghosts, to_near[slots:, :])
    known = near_head[...] + (known + mm(returned, far_near[...])) * scale_of(first_step)
    out[...] = jnp.concatenate([sums, known.astype(BF16)], axis=1)


def advance_kernel(
    first_step, spread, same, send_row, to_own, to_ghost, total, sent, arrived, values, near_ghosts, far_picked, terms, parcel
):
    slots = far_picked.shape[1]
    sums = arrived[:, :slots]
    for i, n in steps(values.shape[1], 256):
        added = mm(sums, spread[0, :, i : i + n]) * scale_of(first_step)
        values[:, i : i + n] = (total[:, i : i + n] + added).astype(BF16)
    near = mm(sent[:, :slots], same[...]) * scale_of(first_step) + arrived[:, slots:].astype(F32)
    near_ghosts[...] = near.astype(BF16)
    terms_kernel(send_row, to_own, values, terms, far_picked)
    parcel_kernel(terms, to_ghost, near_ghosts, far_picked, parcel)


def near_kernel(terms, to_ghost, near_ghosts, parcel, after, out):
    width, slots = out.shape
    arrived = [(0, near_ghosts[:width, :]), (1, parcel[:width, :slots])]
    out[...] = ghost_sum(0, terms, to_ghost, arrived)


def scale_of(first_step):
    return (1.0 if first_step else 2.0) / HALF_WIDTH


def own_kernel(first_step, to_own, head, *refs):
    arrived, out = refs[:-1], refs[-1]
    ghosts = jnp.concatenate([ghost[...] for ghost in arrived], axis=1)
    for i, n in steps(out.shape[1], 256):
        at = slice(i, i + n)
        out[:, at] = head[:, at] + mm(ghosts, to_own[:, at]) * scale_of(first_step)


def paired_own_kernel(
    first_step, to_own, head, spread, near_ghosts, far_picked, parcel, first_parcel, out
):
    width, slots = far_picked.shape
    ghosts = jnp.concatenate([near_ghosts[:width, :], parcel[:width, :slots]], axis=1)
    returned = returned_sums(far_picked, parcel, first_parcel)
    for i, n in steps(out.shape[1], 256):
        at = slice(i, i + n)
        sums = mm(ghosts, to_own[:, at]) + mm(returned, spread[1, :, at])
        out[:, at] = head[:, at] + sums * scale_of(first_step)


def updated_columns(first_step, spread, i, n, total, arrived):
    sums = 0.0
    for block, ghost in enumerate(arrived):
        sums = sums + mm(ghost[...], spread[block, :, i : i + n])
    return (total[:, i : i + n] + sums * scale_of(first_step)).astype(BF16)


def update_kernel(blocks, first_step, spread, send_row, total, *refs):
    arrived, (out, near_picked) = refs[:blocks], refs[blocks:]
    for i, n in steps(out.shape[1], 256):
        out[:, i : i + n] = updated_columns(first_step, spread, i, n, total, arrived)
    near_picked[...] = mm_nt(out[...], spread[0]).astype(BF16)


def last_kernel(blocks, first_step, spread, total, *refs):
    arrived, (out, held, sems) = refs[:blocks], refs[blocks:]
    copies = []
    for part, (i, n) in enumerate(steps(out.shape[1], 256)):
        held[:, i : i + n] = updated_columns(first_step, spread, i, n, total, arrived)
        at = pl.ds(i, n)
        copies.append(pltpu.make_async_copy(held.at[:, at], out.at[:, at], sems.at[part]))
        copies[-1].start()
    for copy in copies:
        copy.wait()


def shards(
    orbitals, rotation, cell_stiffness, cell_scale, potential, cell_nodes, send_rows, domain_rows
):
    domains = lax.axis_size("dom")
    bands = lax.axis_size("band")
    domain = lax.axis_index("dom")
    row_piece = orbitals[0]
    piece_rows, columns = row_piece.shape
    own_rows = domain_rows[0]
    width = columns // bands
    piece_shapes = (shape((width, piece_rows), BF16),) * bands
    pieces = list(call(
        rotate_kernel,
        piece_shapes,
        (row_piece.T, rotation),
        2 * piece_rows * columns * columns,
        scratch=[
            pltpu.VMEM((columns, piece_rows), BF16),
            pltpu.VMEM((columns, columns), BF16),
            pltpu.VMEM((bands, width, piece_rows), BF16),
            pltpu.SemaphoreType.DMA((2,)),
        ],
        in_specs=[ANY, ANY],
        vmem=ROTATE_VMEM,
    ))
    for k in reversed(range(1, bands)):
        pieces[k] = lax.ppermute(pieces[k], "band", [(i, i ^ k) for i in range(bands)])

    capacity = potential.shape[1]
    cells, nodes = cell_nodes.shape[1:]
    slots = send_rows.shape[2]
    nodes_pad = round_up(nodes, 256)
    slots_pad = round_up(slots, 16)
    far = far_groups(domains)
    blocks = 2 + len(far)
    ghosts = blocks * slots_pad
    even = domain % 2 == 0
    send_lists = [
        jnp.where(even, send_rows[0, 3], send_rows[0, 0]),
        jnp.where(even, send_rows[0, 0], send_rows[0, 3]),
    ] + [send_rows[0, g] for g in far]
    send_row = jnp.pad(
        jnp.stack(send_lists), ((0, 0), (0, slots_pad - slots)), constant_values=capacity
    )
    group = (cell_nodes[0] - capacity) // slots
    slot = (cell_nodes[0] - capacity) % slots
    block = jnp.where((group == 0) == even, 0, 1)
    for pos, g in enumerate(far):
        block = jnp.where(group == g, 2 + pos, block)
    ghost_index = capacity + block * slots_pad + slot
    node_list = jnp.where(cell_nodes[0] < capacity, cell_nodes[0], ghost_index)
    node_list = jnp.pad(
        node_list, ((0, 0), (0, nodes_pad - nodes)), constant_values=capacity + ghosts
    ).reshape(-1)
    node_row = node_list[None, :]
    stiffness = jnp.pad(cell_stiffness, ((0, nodes_pad - nodes), (0, nodes_pad - nodes)))

    cell_total = (own_rows - FACE_NODES) // (DEGREE * FACE_NODES)
    cell_live = jnp.arange(cell_scale.shape[1], dtype=jnp.int32) < cell_total
    weight = jnp.where(cell_live, cell_scale[0], jnp.zeros_like(cell_scale[0]))
    weight = jnp.repeat(weight, nodes_pad)[None, :]

    local_rows = cells * nodes_pad
    cell_flops = 2 * local_rows * nodes_pad
    to_ghost, to_own, scatter, spread, to_near, far_near = call(
        functools.partial(couple_kernel, capacity),
        (
            shape((blocks, ghosts, slots_pad), BF16),
            shape((ghosts, capacity), BF16),
            shape((local_rows, capacity), BF16),
            shape((blocks, slots_pad, capacity), BF16),
            shape((ghosts, slots_pad), BF16),
            shape((slots_pad, slots_pad), BF16),
        ),
        (weight, node_row, send_row, stiffness),
        (cell_flops + 2 * local_rows * (ghosts + capacity)) * ghosts,
        scratch=[pltpu.VMEM((ghosts, local_rows), BF16)],
    )
    block_shape = shape((width, slots_pad), BF16)
    keep = (jnp.arange(capacity, dtype=jnp.int32) < own_rows).astype(jnp.int32)[None, :]
    near_rows = width if far else round_up(width, 16) + DIGIT_ROWS
    digits = jnp.pad(
        jnp.stack([send_row[0] // DIGIT, send_row[0] % DIGIT]), ((0, DIGIT_ROWS - 2), (0, 0))
    ).astype(BF16)
    current, near_picked = call(
        join_kernel,
        (shape((width, capacity), BF16), shape((near_rows, slots_pad), BF16)),
        (send_row, keep, digits, to_ghost, *pieces),
        2 * slots_pad * capacity * width,
        scratch=[pltpu.VMEM((bands, width, piece_rows), BF16)],
        in_specs=[VMEM, VMEM, VMEM, ANY] + [VMEM] * bands,
    )
    previous = None
    parcel_rows = round_up(width, 16) + coupling_rows(slots_pad)
    terms_shape = shape((blocks, width, slots_pad), F32)
    terms_flops = 4 * ghosts * capacity * width
    for filter_step in range(FILTER_STEPS):
        first, last = filter_step == 0, filter_step == FILTER_STEPS - 1
        if first or far:
            near = swap(near_picked, 0)
            terms, *picked = call(
                terms_kernel,
                (terms_shape,) + (block_shape,) * (blocks - 1),
                (send_row, to_own, current),
                terms_flops,
            )
        if far:
            arrived = [near, *exchange(picked, False)]
            ready = terms
        else:
            if first:
                same = call(
                    functools.partial(same_kernel, capacity),
                    shape((slots_pad, slots_pad), BF16),
                    (near,),
                    slots_pad * slots_pad,
                )
                ready = call(
                    parcel_kernel,
                    shape((parcel_rows, 2 * slots_pad), BF16),
                    (terms, to_ghost, near, picked[0]),
                    2 * slots_pad * slots_pad * width,
                )
            parcel = swap(ready, 1)
            first_parcel = parcel if first else first_parcel
        history = () if first else (previous,)
        near_wanted = not far and not last
        head, *near_head = call(
            functools.partial(cells_kernel, first, near_wanted),
            (shape((width, capacity), F32),) + (shape((width, slots_pad), F32),) * near_wanted,
            (weight, node_row, stiffness, scatter, spread, potential, current, ready, *history),
            (cell_flops + 4 * local_rows * capacity) * width,
            scratch=[pltpu.VMEM((width, local_rows), BF16)] + [pltpu.VMEM((width, nodes_pad), BF16)] * cells,
            in_specs=[VMEM] * 7 + [ANY] + [VMEM] * len(history),
        )
        own_flops = 2 * capacity * ghosts * width
        if far:
            sums = call(
                ghost_kernel,
                (block_shape,) * blocks,
                (terms, to_ghost, *arrived),
                2 * ghosts * ghosts * width,
            )
            returned = [swap(sums[0], 0), *exchange(sums[1:], True)]
            total = call(
                functools.partial(own_kernel, first),
                shape((width, capacity), F32),
                (to_own, head, *arrived),
                own_flops,
            )
        else:
            if last:
                sent = call(
                    near_kernel,
                    block_shape,
                    (terms, to_ghost, near, parcel, head),
                    2 * ghosts * slots_pad * width,
                    in_specs=[VMEM] * 4 + [ANY],
                )
            else:
                sent = call(
                    functools.partial(pair_kernel, first),
                    shape((width, 2 * slots_pad), BF16),
                    (terms, to_ghost, near, picked[0], parcel, first_parcel, *near_head, to_near, far_near),
                    6 * ghosts * slots_pad * width,
                )
            returned = [swap(sent, 0)]
            total = call(
                functools.partial(paired_own_kernel, first),
                shape((width, capacity), F32),
                (to_own, head, spread, near, picked[0], parcel, first_parcel),
                own_flops,
            )
        update_flops = 2 * capacity * (ghosts + slots_pad * len(returned)) * width
        if last:
            current = call(
                functools.partial(last_kernel, len(returned), first),
                shape((width, capacity), BF16),
                (spread, total, *returned),
                update_flops,
                scratch=[
                    pltpu.VMEM((width, capacity), BF16),
                    pltpu.SemaphoreType.DMA((len(steps(capacity, 256)),)),
                ],
                out_specs=ANY,
            )
        elif not far:
            following, near, far_picked, terms, ready = call(
                functools.partial(advance_kernel, first),
                (
                    shape((width, capacity), BF16),
                    block_shape,
                    block_shape,
                    terms_shape,
                    shape((width, 2 * slots_pad), BF16),
                ),
                (spread, same, send_row, to_own, to_ghost, total, sent, *returned),
                update_flops + terms_flops,
            )
            picked = [far_picked]
            previous, current = current, following
        else:
            following, near_picked = call(
                functools.partial(update_kernel, len(returned), first),
                (shape((width, capacity), BF16), block_shape),
                (spread, send_row, total, *returned),
                update_flops,
            )
            previous, current = current, following
    return current.T[None]


def solution(mesh):
    return jax.shard_map(
        shards,
        mesh=mesh,
        in_specs=(
            P("dom", "band", None),
            P(),
            P(),
            P("dom", None),
            P("dom", None),
            P("dom", None, None),
            P("dom", None, None),
            P("dom"),
        ),
        out_specs=P("dom", None, "band"),
        check_vma=False,
    )
```

```python
import functools

import jax
import jax.numpy as jnp
from jax import lax
from jax.experimental import pallas as pl
from jax.experimental.pallas import tpu as pltpu
from jax.sharding import PartitionSpec as P

DEGREE = 8
FILTER_STEPS = 3
FACE_NODES = 81

OFFSETS = (1, 8, -8, -1)
CENTER = 5.0
HALF_WIDTH = 5.0
BF16 = jnp.bfloat16
F32 = jnp.float32
VMEM = pl.BlockSpec(memory_space=pltpu.VMEM)
ANY = pl.BlockSpec(memory_space=pl.ANY)
LANES = 128
DIGIT = 64
DIGIT_ROWS = 16
ROTATE_VMEM = 53 << 20


def round_up(value, multiple):
    return -(-value // multiple) * multiple


def swap(value, first):
    domains = lax.axis_size("dom")
    pairs = []
    for low in range(first, domains - 1, 2):
        pairs += [(low, low + 1), (low + 1, low)]
    return lax.ppermute(value, "dom", pairs)


def shift(value, by):
    domains = lax.axis_size("dom")
    pairs = [(i, i + by) for i in range(domains) if 0 <= i + by < domains]
    return lax.ppermute(value, "dom", pairs)


def far_groups(domains):
    return [g for g, offset in enumerate(OFFSETS) if abs(offset) > 1 and abs(offset) < domains]


def exchange(blocks, to_owner):
    out = [swap(blocks[0], 1)]
    for block, group in zip(blocks[1:], far_groups(lax.axis_size("dom"))):
        out.append(shift(block, OFFSETS[group] if to_owner else -OFFSETS[group]))
    return out


def call(kernel, out_shape, args, flops, scratch=(), in_specs=None, out_specs=None, vmem=16 << 20):
    outs = out_shape if isinstance(out_shape, (tuple, list)) else (out_shape,)
    size = sum(a.size * a.dtype.itemsize for a in list(args) + list(outs))
    return pl.pallas_call(
        kernel,
        out_shape=out_shape,
        in_specs=in_specs or [VMEM] * len(args),
        out_specs=out_specs or jax.tree.map(lambda _: VMEM, out_shape),
        scratch_shapes=list(scratch),
        cost_estimate=pl.CostEstimate(flops=flops, bytes_accessed=size, transcendentals=0),
        compiler_params=pltpu.CompilerParams(vmem_limit_bytes=vmem),
    )(*args)


def shape(dims, dtype):
    return jax.ShapeDtypeStruct(dims, dtype)


def mm(a, b):
    return jnp.dot(a, b, preferred_element_type=F32)


def mm_nt(a, b):
    return lax.dot_general(a, b, (((1,), (1,)), ((), ())), preferred_element_type=F32)


def rows_hot(index, first, count):
    rows = lax.broadcasted_iota(jnp.int32, (count, index.shape[1]), 0) + first
    return (rows == index).astype(BF16)


def steps(total, size):
    return [(i, min(size, total - i)) for i in range(0, total, size)]


def rotate_kernel(piece, rotation, *refs):
    outs, (piece_held, rotation_held, groups, sems) = refs[:-4], refs[-4:]
    copies = (
        pltpu.make_async_copy(rotation, rotation_held, sems.at[0]),
        pltpu.make_async_copy(piece, piece_held, sems.at[1]),
    )
    for copy in copies:
        copy.start()
    for copy in copies:
        copy.wait()
    rotated = lax.dot_general(
        rotation_held[...], piece_held[...], (((0,), (0,)), ((), ())), preferred_element_type=F32
    )
    width = groups.shape[1]
    for group in range(groups.shape[0]):
        groups[group] = rotated[group * width : (group + 1) * width, :].astype(BF16)
    mine = lax.axis_index("band")
    for k, out in enumerate(outs):
        out[...] = groups[mine ^ k]


def columns_hot(index, capacity, hot):
    turned = jnp.broadcast_to(index, (LANES, index.shape[1])).T
    for i, n in steps(capacity, LANES):
        lanes = lax.broadcasted_iota(jnp.int32, (turned.shape[0], n), 1) + i
        hot[:, i : i + n] = (turned[:, :n] == lanes).astype(BF16)


def couple_kernel(capacity, weight, node_row, send_row, stiffness, to_ghost, to_own, scatter, spread, far_near, pairing, local):
    nodes = stiffness.shape[0]
    ghosts = to_own.shape[0]
    slots = to_ghost.shape[2]
    for i, n in steps(node_row.shape[1], nodes):
        picks = rows_hot(node_row[:, i : i + n], capacity, ghosts)
        local[:, i : i + n] = (mm(picks, stiffness[...]) * weight[:, i : i + n]).astype(BF16)
    columns_hot(node_row[...], capacity, scatter)
    for block in range(to_ghost.shape[0]):
        columns_hot(send_row[block : block + 1, :], capacity, spread.at[block])
    for block in range(to_ghost.shape[0]):
        picks = rows_hot(node_row[...], capacity + block * slots, slots)
        to_ghost[block] = mm_nt(local[...], picks).astype(BF16)
    for i, n in steps(capacity, 256):
        to_own[:, i : i + n] = mm(local[...], scatter[:, i : i + n]).astype(BF16)
    far_near[...] = mm_nt(spread[1], spread[0]).astype(BF16)
    both = 2 * slots
    to_near = mm_nt(to_own[:both, :], spread[0]).astype(BF16)
    pairing[:both, :] = jnp.concatenate([to_ghost[0, :both, :], to_near], axis=1)
    pairing[both:, :] = jnp.concatenate([jnp.zeros((slots, slots), BF16), far_near[...]], axis=1)


def same_kernel(capacity, first_near, same):
    slots = same.shape[0]
    digits = first_near[first_near.shape[0] - DIGIT_ROWS :, :].astype(F32)
    rows = digits[0:1, :] * DIGIT + digits[1:2, :]
    turned = jnp.broadcast_to(rows, (slots, slots)).T
    same[...] = ((turned == rows) & (turned < capacity)).astype(BF16)


def pick_rows(send_row, block, values, out):
    picks = rows_hot(send_row[block : block + 1, :], 0, values.shape[1])
    out[: values.shape[0], :] = mm(values[...], picks).astype(BF16)


def join_kernel(send_row, keep, digits, after, *refs):
    bands = refs[-1].shape[0]
    pieces, (values, near_picked, held) = refs[:bands], refs[bands:]
    mine = lax.axis_index("band")
    for k, piece in enumerate(pieces):
        held[mine ^ k] = piece[...]
    joined = jnp.concatenate([held[p] for p in range(bands)], axis=1)
    values[...] = jnp.where(keep[...] > 0, joined.astype(F32), 0.0).astype(BF16)
    if near_picked.shape[0] > values.shape[0]:
        near_picked[...] = jnp.zeros(near_picked.shape, BF16)
        near_picked[near_picked.shape[0] - DIGIT_ROWS :, :] = digits[...]
    pick_rows(send_row, 0, values, near_picked)


def terms_kernel(send_row, to_own, values, terms, *picked):
    slots = terms.shape[2]
    for block, out in enumerate(picked):
        pick_rows(send_row, block + 1, values, out)
    for block in range(terms.shape[0]):
        terms[block] = mm_nt(values[...], to_own[block * slots : (block + 1) * slots, :])


def cells_kernel(first_step, near_wanted, weight, node_row, stiffness, scatter, spread, potential, values, after, *refs):
    refs = list(refs)
    previous = None if first_step else refs.pop(0)
    terms = refs.pop(0) if near_wanted else None
    out = refs.pop(0)
    near_out = refs.pop(0) if near_wanted else None
    product, *locals_ = refs
    capacity = values.shape[1]
    nodes = stiffness.shape[0]
    parts = steps(product.shape[1], nodes)
    for (i, n), local in zip(parts, locals_):
        local[...] = mm(values[...], rows_hot(node_row[:, i : i + n], 0, capacity)).astype(BF16)
    for (i, n), local in zip(parts, locals_):
        product[:, i : i + n] = (mm(local[...], stiffness[...]) * weight[:, i : i + n]).astype(BF16)
    for i, n in steps(capacity, 256):
        at = slice(i, i + n)
        sums = mm(product[...], scatter[:, at])
        shifted = sums + (potential[:, at] - CENTER) * values[:, at].astype(F32)
        result = shifted * scale_of(first_step)
        out[:, at] = result if first_step else result - previous[:, at].astype(F32)
    if near_wanted:
        near_head = mm_nt(out[...].astype(BF16), spread[0])
        near_out[...] = jnp.concatenate([terms[0], near_head], axis=1)


def ghost_sum(block, terms, to_ghost, arrived):
    slots = terms.shape[2]
    total = terms[block]
    for other, values in arrived:
        total = total + mm(values, to_ghost[block, other * slots : (other + 1) * slots, :])
    return total.astype(BF16)


def ghost_kernel(terms, to_ghost, *refs):
    blocks = terms.shape[0]
    arrived = [(other, refs[other][...]) for other in range(blocks)]
    for block in range(blocks):
        refs[blocks + block][...] = ghost_sum(block, terms, to_ghost, arrived)


def coupling_rows(slots):
    return round_up(-(-slots // 2), 16)


def parcel_kernel(terms, to_ghost, near_ghosts, far_picked, parcel):
    width, slots = far_picked.shape
    sums = ghost_sum(1, terms, to_ghost, [(0, near_ghosts[:width, :])])
    if parcel.shape[0] > width:
        half = coupling_rows(slots)
        first = parcel.shape[0] - half
        parcel[...] = jnp.zeros(parcel.shape, BF16)
        parcel[first:, :slots] = to_ghost[1, slots : slots + half, :]
        parcel[first : first + slots - half, slots:] = to_ghost[1, slots + half : 2 * slots, :]
    parcel[:width, :] = jnp.concatenate([far_picked[...], sums], axis=1)


def unpacked_coupling(first_parcel, slots):
    half = coupling_rows(slots)
    start = first_parcel.shape[0] - half
    return jnp.concatenate(
        [first_parcel[start:, :slots], first_parcel[start : start + slots - half, slots:]], axis=0
    )


def returned_sums(far_picked, parcel, first_parcel):
    width, slots = far_picked.shape
    coupling = unpacked_coupling(first_parcel, slots)
    returned = parcel[:width, slots:].astype(F32) + mm(far_picked[...], coupling)
    return returned.astype(BF16)


def pair_kernel(first_step, near_ghosts, far_picked, parcel, near_head, pairing, coupling, *refs):
    width, slots = far_picked.shape
    if first_step:
        far_near, out, coupled = refs
        added = mm(unpacked_coupling(coupling, slots), far_near[...]).astype(BF16)
        coupled[...] = jnp.concatenate([jnp.zeros((slots, slots), BF16), added], axis=1)
    else:
        (out,), coupled = refs, coupling
    both = mm(near_ghosts[:width, :], pairing[:slots, :])
    both = both + mm(parcel[:width, :], pairing[slots:, :]) + mm(far_picked[...], coupled[...])
    lanes = lax.broadcasted_iota(jnp.int32, (1, 2 * slots), 1)
    scale = jnp.where(lanes < slots, 1.0, scale_of(first_step))
    out[...] = (near_head[...] + both * scale).astype(BF16)


def advance_kernel(
    first_step, spread, same, send_row, to_own, to_ghost, total, sent, arrived, values, near_ghosts, far_picked, terms, parcel
):
    slots = far_picked.shape[1]
    sums = arrived[:, :slots]
    for i, n in steps(values.shape[1], 256):
        added = mm(sums, spread[0, :, i : i + n]) * scale_of(first_step)
        values[:, i : i + n] = (total[:, i : i + n] + added).astype(BF16)
    near = mm(sent[:, :slots], same[...]) * scale_of(first_step) + arrived[:, slots:].astype(F32)
    near_ghosts[...] = near.astype(BF16)
    terms_kernel(send_row, to_own, values, terms, far_picked)
    parcel_kernel(terms, to_ghost, near_ghosts, far_picked, parcel)


def near_kernel(terms, to_ghost, near_ghosts, parcel, after, out):
    width, slots = out.shape
    arrived = [(0, near_ghosts[:width, :]), (1, parcel[:width, :slots])]
    out[...] = ghost_sum(0, terms, to_ghost, arrived)


def scale_of(first_step):
    return (1.0 if first_step else 2.0) / HALF_WIDTH


def own_kernel(first_step, to_own, head, *refs):
    arrived, out = refs[:-1], refs[-1]
    ghosts = jnp.concatenate([ghost[...] for ghost in arrived], axis=1)
    for i, n in steps(out.shape[1], 256):
        at = slice(i, i + n)
        out[:, at] = head[:, at] + mm(ghosts, to_own[:, at]) * scale_of(first_step)


def paired_own_kernel(
    first_step, to_own, head, spread, near_ghosts, far_picked, parcel, first_parcel, out
):
    width, slots = far_picked.shape
    ghosts = jnp.concatenate([near_ghosts[:width, :], parcel[:width, :slots]], axis=1)
    returned = returned_sums(far_picked, parcel, first_parcel)
    for i, n in steps(out.shape[1], 256):
        at = slice(i, i + n)
        sums = mm(ghosts, to_own[:, at]) + mm(returned, spread[1, :, at])
        out[:, at] = head[:, at] + sums * scale_of(first_step)


def updated_columns(first_step, spread, i, n, total, arrived):
    sums = 0.0
    for block, ghost in enumerate(arrived):
        sums = sums + mm(ghost[...], spread[block, :, i : i + n])
    return (total[:, i : i + n] + sums * scale_of(first_step)).astype(BF16)


def update_kernel(blocks, first_step, spread, send_row, total, *refs):
    arrived, (out, near_picked) = refs[:blocks], refs[blocks:]
    for i, n in steps(out.shape[1], 256):
        out[:, i : i + n] = updated_columns(first_step, spread, i, n, total, arrived)
    near_picked[...] = mm_nt(out[...], spread[0]).astype(BF16)


def last_kernel(blocks, first_step, spread, total, *refs):
    arrived, (out, held, sems) = refs[:blocks], refs[blocks:]
    copies = []
    for part, (i, n) in enumerate(steps(out.shape[1], 256)):
        held[:, i : i + n] = updated_columns(first_step, spread, i, n, total, arrived)
        at = pl.ds(i, n)
        copies.append(pltpu.make_async_copy(held.at[:, at], out.at[:, at], sems.at[part]))
        copies[-1].start()
    for copy in copies:
        copy.wait()


def shards(
    orbitals, rotation, cell_stiffness, cell_scale, potential, cell_nodes, send_rows, domain_rows
):
    domains = lax.axis_size("dom")
    bands = lax.axis_size("band")
    domain = lax.axis_index("dom")
    row_piece = orbitals[0]
    piece_rows, columns = row_piece.shape
    own_rows = domain_rows[0]
    width = columns // bands
    piece_shapes = (shape((width, piece_rows), BF16),) * bands
    pieces = list(call(
        rotate_kernel,
        piece_shapes,
        (row_piece.T, rotation),
        2 * piece_rows * columns * columns,
        scratch=[
            pltpu.VMEM((columns, piece_rows), BF16),
            pltpu.VMEM((columns, columns), BF16),
            pltpu.VMEM((bands, width, piece_rows), BF16),
            pltpu.SemaphoreType.DMA((2,)),
        ],
        in_specs=[ANY, ANY],
        vmem=ROTATE_VMEM,
    ))
    for k in reversed(range(1, bands)):
        pieces[k] = lax.ppermute(pieces[k], "band", [(i, i ^ k) for i in range(bands)])

    capacity = potential.shape[1]
    cells, nodes = cell_nodes.shape[1:]
    slots = send_rows.shape[2]
    nodes_pad = round_up(nodes, 256)
    slots_pad = round_up(slots, 16)
    far = far_groups(domains)
    blocks = 2 + len(far)
    ghosts = blocks * slots_pad
    even = domain % 2 == 0
    send_lists = [
        jnp.where(even, send_rows[0, 3], send_rows[0, 0]),
        jnp.where(even, send_rows[0, 0], send_rows[0, 3]),
    ] + [send_rows[0, g] for g in far]
    send_row = jnp.pad(
        jnp.stack(send_lists), ((0, 0), (0, slots_pad - slots)), constant_values=capacity
    )
    group = (cell_nodes[0] - capacity) // slots
    slot = (cell_nodes[0] - capacity) % slots
    block = jnp.where((group == 0) == even, 0, 1)
    for pos, g in enumerate(far):
        block = jnp.where(group == g, 2 + pos, block)
    ghost_index = capacity + block * slots_pad + slot
    node_list = jnp.where(cell_nodes[0] < capacity, cell_nodes[0], ghost_index)
    node_list = jnp.pad(
        node_list, ((0, 0), (0, nodes_pad - nodes)), constant_values=capacity + ghosts
    ).reshape(-1)
    node_row = node_list[None, :]
    stiffness = jnp.pad(cell_stiffness, ((0, nodes_pad - nodes), (0, nodes_pad - nodes)))

    cell_total = (own_rows - FACE_NODES) // (DEGREE * FACE_NODES)
    cell_live = jnp.arange(cell_scale.shape[1], dtype=jnp.int32) < cell_total
    weight = jnp.where(cell_live, cell_scale[0], jnp.zeros_like(cell_scale[0]))
    weight = jnp.repeat(weight, nodes_pad)[None, :]

    local_rows = cells * nodes_pad
    cell_flops = 2 * local_rows * nodes_pad
    to_ghost, to_own, scatter, spread, far_near, pairing = call(
        functools.partial(couple_kernel, capacity),
        (
            shape((blocks, ghosts, slots_pad), BF16),
            shape((ghosts, capacity), BF16),
            shape((local_rows, capacity), BF16),
            shape((blocks, slots_pad, capacity), BF16),
            shape((slots_pad, slots_pad), BF16),
            shape((3 * slots_pad, 2 * slots_pad), BF16),
        ),
        (weight, node_row, send_row, stiffness),
        (cell_flops + 2 * local_rows * (ghosts + capacity)) * ghosts,
        scratch=[pltpu.VMEM((ghosts, local_rows), BF16)],
    )
    block_shape = shape((width, slots_pad), BF16)
    keep = (jnp.arange(capacity, dtype=jnp.int32) < own_rows).astype(jnp.int32)[None, :]
    near_rows = width if far else round_up(width, 16) + DIGIT_ROWS
    digits = jnp.pad(
        jnp.stack([send_row[0] // DIGIT, send_row[0] % DIGIT]), ((0, DIGIT_ROWS - 2), (0, 0))
    ).astype(BF16)
    current, near_picked = call(
        join_kernel,
        (shape((width, capacity), BF16), shape((near_rows, slots_pad), BF16)),
        (send_row, keep, digits, to_ghost, *pieces),
        2 * slots_pad * capacity * width,
        scratch=[pltpu.VMEM((bands, width, piece_rows), BF16)],
        in_specs=[VMEM, VMEM, VMEM, ANY] + [VMEM] * bands,
    )
    previous = None
    parcel_rows = round_up(width, 16) + coupling_rows(slots_pad)
    terms_shape = shape((blocks, width, slots_pad), F32)
    terms_flops = 4 * ghosts * capacity * width
    for filter_step in range(FILTER_STEPS):
        first, last = filter_step == 0, filter_step == FILTER_STEPS - 1
        if first or far:
            near = swap(near_picked, 0)
            terms, *picked = call(
                terms_kernel,
                (terms_shape,) + (block_shape,) * (blocks - 1),
                (send_row, to_own, current),
                terms_flops,
            )
        if far:
            arrived = [near, *exchange(picked, False)]
            ready = terms
        else:
            if first:
                same = call(
                    functools.partial(same_kernel, capacity),
                    shape((slots_pad, slots_pad), BF16),
                    (near,),
                    slots_pad * slots_pad,
                )
                ready = call(
                    parcel_kernel,
                    shape((parcel_rows, 2 * slots_pad), BF16),
                    (terms, to_ghost, near, picked[0]),
                    2 * slots_pad * slots_pad * width,
                )
            parcel = swap(ready, 1)
            first_parcel = parcel if first else first_parcel
        history = () if first else (previous,)
        near_wanted = not far and not last
        wanted = (terms,) if near_wanted else ()
        head, *near_head = call(
            functools.partial(cells_kernel, first, near_wanted),
            (shape((width, capacity), F32),) + (shape((width, 2 * slots_pad), F32),) * near_wanted,
            (weight, node_row, stiffness, scatter, spread, potential, current, ready, *history, *wanted),
            (cell_flops + 4 * local_rows * capacity) * width,
            scratch=[pltpu.VMEM((width, local_rows), BF16)] + [pltpu.VMEM((width, nodes_pad), BF16)] * cells,
            in_specs=[VMEM] * 7 + [ANY] + [VMEM] * len((*history, *wanted)),
        )
        own_flops = 2 * capacity * ghosts * width
        if far:
            sums = call(
                ghost_kernel,
                (block_shape,) * blocks,
                (terms, to_ghost, *arrived),
                2 * ghosts * ghosts * width,
            )
            returned = [swap(sums[0], 0), *exchange(sums[1:], True)]
            total = call(
                functools.partial(own_kernel, first),
                shape((width, capacity), F32),
                (to_own, head, *arrived),
                own_flops,
            )
        else:
            if last:
                sent = call(
                    near_kernel,
                    block_shape,
                    (terms, to_ghost, near, parcel, head),
                    2 * ghosts * slots_pad * width,
                    in_specs=[VMEM] * 4 + [ANY],
                )
            else:
                sent_shape = shape((width, 2 * slots_pad), BF16)
                coupled_shape = shape((slots_pad, 2 * slots_pad), BF16)
                sent, *coupled_out = call(
                    functools.partial(pair_kernel, first),
                    (sent_shape, coupled_shape) if first else (sent_shape,),
                    (near, picked[0], parcel, *near_head, pairing)
                    + ((first_parcel, far_near) if first else (coupled,)),
                    8 * ghosts * slots_pad * width,
                )
                coupled = coupled_out[0] if first else coupled
            returned = [swap(sent, 0)]
            total = call(
                functools.partial(paired_own_kernel, first),
                shape((width, capacity), F32),
                (to_own, head, spread, near, picked[0], parcel, first_parcel),
                own_flops,
            )
        update_flops = 2 * capacity * (ghosts + slots_pad * len(returned)) * width
        if last:
            current = call(
                functools.partial(last_kernel, len(returned), first),
                shape((width, capacity), BF16),
                (spread, total, *returned),
                update_flops,
                scratch=[
                    pltpu.VMEM((width, capacity), BF16),
                    pltpu.SemaphoreType.DMA((len(steps(capacity, 256)),)),
                ],
                out_specs=ANY,
            )
        elif not far:
            following, near, far_picked, terms, ready = call(
                functools.partial(advance_kernel, first),
                (
                    shape((width, capacity), BF16),
                    block_shape,
                    block_shape,
                    terms_shape,
                    shape((width, 2 * slots_pad), BF16),
                ),
                (spread, same, send_row, to_own, to_ghost, total, sent, *returned),
                update_flops + terms_flops,
            )
            picked = [far_picked]
            previous, current = current, following
        else:
            following, near_picked = call(
                functools.partial(update_kernel, len(returned), first),
                (shape((width, capacity), BF16), block_shape),
                (spread, send_row, total, *returned),
                update_flops,
            )
            previous, current = current, following
    return current.T[None]


def solution(mesh):
    return jax.shard_map(
        shards,
        mesh=mesh,
        in_specs=(
            P("dom", "band", None),
            P(),
            P(),
            P("dom", None),
            P("dom", None),
            P("dom", None, None),
            P("dom", None, None),
            P("dom"),
        ),
        out_specs=P("dom", None, "band"),
        check_vma=False,
    )
```

```python
import functools

import jax
import jax.numpy as jnp
from jax import lax
from jax.experimental import pallas as pl
from jax.experimental.pallas import tpu as pltpu
from jax.sharding import PartitionSpec as P

DEGREE = 8
FILTER_STEPS = 3
FACE_NODES = 81

OFFSETS = (1, 8, -8, -1)
CENTER = 5.0
HALF_WIDTH = 5.0
BF16 = jnp.bfloat16
F32 = jnp.float32
VMEM = pl.BlockSpec(memory_space=pltpu.VMEM)
ANY = pl.BlockSpec(memory_space=pl.ANY)
LANES = 128
DIGIT = 64
LAST_COLUMNS = 512
DIGIT_ROWS = 16
ROTATE_VMEM = 53 << 20


def round_up(value, multiple):
    return -(-value // multiple) * multiple


def swap(value, first):
    domains = lax.axis_size("dom")
    pairs = []
    for low in range(first, domains - 1, 2):
        pairs += [(low, low + 1), (low + 1, low)]
    return lax.ppermute(value, "dom", pairs)


def shift(value, by):
    domains = lax.axis_size("dom")
    pairs = [(i, i + by) for i in range(domains) if 0 <= i + by < domains]
    return lax.ppermute(value, "dom", pairs)


def far_groups(domains):
    return [g for g, offset in enumerate(OFFSETS) if abs(offset) > 1 and abs(offset) < domains]


def exchange(blocks, to_owner):
    out = [swap(blocks[0], 1)]
    for block, group in zip(blocks[1:], far_groups(lax.axis_size("dom"))):
        out.append(shift(block, OFFSETS[group] if to_owner else -OFFSETS[group]))
    return out


def call(kernel, out_shape, args, flops, scratch=(), in_specs=None, out_specs=None, vmem=16 << 20):
    outs = out_shape if isinstance(out_shape, (tuple, list)) else (out_shape,)
    size = sum(a.size * a.dtype.itemsize for a in list(args) + list(outs))
    return pl.pallas_call(
        kernel,
        out_shape=out_shape,
        in_specs=in_specs or [VMEM] * len(args),
        out_specs=out_specs or jax.tree.map(lambda _: VMEM, out_shape),
        scratch_shapes=list(scratch),
        cost_estimate=pl.CostEstimate(flops=flops, bytes_accessed=size, transcendentals=0),
        compiler_params=pltpu.CompilerParams(vmem_limit_bytes=vmem),
    )(*args)


def shape(dims, dtype):
    return jax.ShapeDtypeStruct(dims, dtype)


def mm(a, b):
    return jnp.dot(a, b, preferred_element_type=F32)


def mm_nt(a, b):
    return lax.dot_general(a, b, (((1,), (1,)), ((), ())), preferred_element_type=F32)


def rows_hot(index, first, count):
    rows = lax.broadcasted_iota(jnp.int32, (count, index.shape[1]), 0) + first
    return (rows == index).astype(BF16)


def steps(total, size):
    return [(i, min(size, total - i)) for i in range(0, total, size)]


def rotate_kernel(piece, rotation, *refs):
    outs, (piece_held, rotation_held, groups, sems) = refs[:-4], refs[-4:]
    copies = (
        pltpu.make_async_copy(rotation, rotation_held, sems.at[0]),
        pltpu.make_async_copy(piece, piece_held, sems.at[1]),
    )
    for copy in copies:
        copy.start()
    for copy in copies:
        copy.wait()
    rotated = lax.dot_general(
        rotation_held[...], piece_held[...], (((0,), (0,)), ((), ())), preferred_element_type=F32
    )
    width = groups.shape[1]
    for group in range(groups.shape[0]):
        groups[group] = rotated[group * width : (group + 1) * width, :].astype(BF16)
    mine = lax.axis_index("band")
    for k, out in enumerate(outs):
        out[...] = groups[mine ^ k]


def columns_hot(index, capacity, hot):
    turned = jnp.broadcast_to(index, (LANES, index.shape[1])).T
    for i, n in steps(capacity, LANES):
        lanes = lax.broadcasted_iota(jnp.int32, (turned.shape[0], n), 1) + i
        hot[:, i : i + n] = (turned[:, :n] == lanes).astype(BF16)


def couple_kernel(capacity, weight, node_row, send_row, stiffness, to_ghost, to_own, scatter, spread, far_near, pairing, local):
    nodes = stiffness.shape[0]
    ghosts = to_own.shape[0]
    slots = to_ghost.shape[2]
    for i, n in steps(node_row.shape[1], nodes):
        picks = rows_hot(node_row[:, i : i + n], capacity, ghosts)
        local[:, i : i + n] = (mm(picks, stiffness[...]) * weight[:, i : i + n]).astype(BF16)
    columns_hot(node_row[...], capacity, scatter)
    for block in range(to_ghost.shape[0]):
        columns_hot(send_row[block : block + 1, :], capacity, spread.at[block])
    for block in range(to_ghost.shape[0]):
        picks = rows_hot(node_row[...], capacity + block * slots, slots)
        to_ghost[block] = mm_nt(local[...], picks).astype(BF16)
    for i, n in steps(capacity, 256):
        to_own[:, i : i + n] = mm(local[...], scatter[:, i : i + n]).astype(BF16)
    far_near[...] = mm_nt(spread[1], spread[0]).astype(BF16)
    both = 2 * slots
    to_near = mm_nt(to_own[:both, :], spread[0]).astype(BF16)
    pairing[:both, :] = jnp.concatenate([to_ghost[0, :both, :], to_near], axis=1)
    pairing[both:, :] = jnp.concatenate([jnp.zeros((slots, slots), BF16), far_near[...]], axis=1)


def same_kernel(capacity, first_near, same):
    slots = same.shape[0]
    digits = first_near[first_near.shape[0] - DIGIT_ROWS :, :].astype(F32)
    rows = digits[0:1, :] * DIGIT + digits[1:2, :]
    turned = jnp.broadcast_to(rows, (slots, slots)).T
    same[...] = ((turned == rows) & (turned < capacity)).astype(BF16)


def pick_rows(send_row, block, values, out):
    picks = rows_hot(send_row[block : block + 1, :], 0, values.shape[1])
    out[: values.shape[0], :] = mm(values[...], picks).astype(BF16)


def join_kernel(send_row, keep, digits, after, *refs):
    bands = refs[-1].shape[0]
    pieces, (values, near_picked, held) = refs[:bands], refs[bands:]
    mine = lax.axis_index("band")
    for k, piece in enumerate(pieces):
        held[mine ^ k] = piece[...]
    joined = jnp.concatenate([held[p] for p in range(bands)], axis=1)
    values[...] = jnp.where(keep[...] > 0, joined.astype(F32), 0.0).astype(BF16)
    if near_picked.shape[0] > values.shape[0]:
        near_picked[...] = jnp.zeros(near_picked.shape, BF16)
        near_picked[near_picked.shape[0] - DIGIT_ROWS :, :] = digits[...]
    pick_rows(send_row, 0, values, near_picked)


def terms_kernel(spread, to_own, values, terms, *picked):
    slots = terms.shape[2]
    for block, out in enumerate(picked):
        out[...] = mm_nt(values[...], spread[block + 1]).astype(BF16)
    for block in range(terms.shape[0]):
        terms[block] = mm_nt(values[...], to_own[block * slots : (block + 1) * slots, :])


def cells_kernel(first_step, near_wanted, weight, node_row, stiffness, scatter, spread, potential, values, after, *refs):
    refs = list(refs)
    previous = None if first_step else refs.pop(0)
    terms = refs.pop(0) if near_wanted else None
    out = refs.pop(0)
    near_out = refs.pop(0) if near_wanted else None
    product, *locals_ = refs
    capacity = values.shape[1]
    nodes = stiffness.shape[0]
    parts = steps(product.shape[1], nodes)
    for (i, n), local in zip(parts, locals_):
        local[...] = mm(values[...], rows_hot(node_row[:, i : i + n], 0, capacity)).astype(BF16)
    for (i, n), local in zip(parts, locals_):
        product[:, i : i + n] = (mm(local[...], stiffness[...]) * weight[:, i : i + n]).astype(BF16)
    for i, n in steps(capacity, 256):
        at = slice(i, i + n)
        sums = mm(product[...], scatter[:, at])
        shifted = sums + (potential[:, at] - CENTER) * values[:, at].astype(F32)
        result = shifted * scale_of(first_step)
        out[:, at] = result if first_step else result - previous[:, at].astype(F32)
    if near_wanted:
        near_head = mm_nt(out[...].astype(BF16), spread[0])
        near_out[...] = jnp.concatenate([terms[0], near_head], axis=1)


def ghost_sum(block, terms, to_ghost, arrived):
    slots = terms.shape[2]
    total = terms[block]
    for other, values in arrived:
        total = total + mm(values, to_ghost[block, other * slots : (other + 1) * slots, :])
    return total.astype(BF16)


def ghost_kernel(terms, to_ghost, *refs):
    blocks = terms.shape[0]
    arrived = [(other, refs[other][...]) for other in range(blocks)]
    for block in range(blocks):
        refs[blocks + block][...] = ghost_sum(block, terms, to_ghost, arrived)


def coupling_rows(slots):
    return round_up(-(-slots // 2), 16)


def parcel_kernel(terms, to_ghost, near_ghosts, far_picked, parcel):
    width, slots = far_picked.shape
    sums = ghost_sum(1, terms, to_ghost, [(0, near_ghosts[:width, :])])
    if parcel.shape[0] > width:
        half = coupling_rows(slots)
        first = parcel.shape[0] - half
        parcel[...] = jnp.zeros(parcel.shape, BF16)
        parcel[first:, :slots] = to_ghost[1, slots : slots + half, :]
        parcel[first : first + slots - half, slots:] = to_ghost[1, slots + half : 2 * slots, :]
    parcel[:width, :] = jnp.concatenate([far_picked[...], sums], axis=1)


def unpacked_coupling(first_parcel, slots):
    half = coupling_rows(slots)
    start = first_parcel.shape[0] - half
    return jnp.concatenate(
        [first_parcel[start:, :slots], first_parcel[start : start + slots - half, slots:]], axis=0
    )


def returned_sums(far_picked, parcel, first_parcel):
    width, slots = far_picked.shape
    coupling = unpacked_coupling(first_parcel, slots)
    returned = parcel[:width, slots:].astype(F32) + mm(far_picked[...], coupling)
    return returned.astype(BF16)


def pair_kernel(first_step, near_ghosts, far_picked, parcel, near_head, pairing, coupling, *refs):
    width, slots = far_picked.shape
    if first_step:
        far_near, out, coupled = refs
        added = mm(unpacked_coupling(coupling, slots), far_near[...]).astype(BF16)
        coupled[...] = jnp.concatenate([jnp.zeros((slots, slots), BF16), added], axis=1)
    else:
        (out,), coupled = refs, coupling
    both = mm(near_ghosts[:width, :], pairing[:slots, :])
    both = both + mm(parcel[:width, :], pairing[slots:, :]) + mm(far_picked[...], coupled[...])
    lanes = lax.broadcasted_iota(jnp.int32, (1, 2 * slots), 1)
    scale = jnp.where(lanes < slots, 1.0, scale_of(first_step))
    out[...] = (near_head[...] + both * scale).astype(BF16)


def advance_kernel(
    first_step, spread, same, to_own, to_ghost, total, sent, arrived, values, near_ghosts, far_picked, terms, parcel
):
    slots = far_picked.shape[1]
    sums = arrived[:, :slots]
    for i, n in steps(values.shape[1], 256):
        added = mm(sums, spread[0, :, i : i + n]) * scale_of(first_step)
        values[:, i : i + n] = (total[:, i : i + n] + added).astype(BF16)
    near = mm(sent[:, :slots], same[...]) * scale_of(first_step) + arrived[:, slots:].astype(F32)
    near_ghosts[...] = near.astype(BF16)
    terms_kernel(spread, to_own, values, terms, far_picked)
    parcel_kernel(terms, to_ghost, near_ghosts, far_picked, parcel)


def near_kernel(terms, to_ghost, near_ghosts, parcel, after, out):
    width, slots = out.shape
    arrived = [(0, near_ghosts[:width, :]), (1, parcel[:width, :slots])]
    out[...] = ghost_sum(0, terms, to_ghost, arrived)


def scale_of(first_step):
    return (1.0 if first_step else 2.0) / HALF_WIDTH


def own_kernel(first_step, to_own, head, *refs):
    arrived, out = refs[:-1], refs[-1]
    ghosts = jnp.concatenate([ghost[...] for ghost in arrived], axis=1)
    for i, n in steps(out.shape[1], 256):
        at = slice(i, i + n)
        out[:, at] = head[:, at] + mm(ghosts, to_own[:, at]) * scale_of(first_step)


def paired_own_kernel(
    first_step, to_own, head, spread, near_ghosts, far_picked, parcel, first_parcel, out
):
    width, slots = far_picked.shape
    ghosts = jnp.concatenate([near_ghosts[:width, :], parcel[:width, :slots]], axis=1)
    returned = returned_sums(far_picked, parcel, first_parcel)
    for i, n in steps(out.shape[1], 256):
        at = slice(i, i + n)
        sums = mm(ghosts, to_own[:, at]) + mm(returned, spread[1, :, at])
        out[:, at] = head[:, at] + sums * scale_of(first_step)


def updated_columns(first_step, spread, i, n, total, arrived):
    sums = 0.0
    for block, ghost in enumerate(arrived):
        sums = sums + mm(ghost[...], spread[block, :, i : i + n])
    return (total[:, i : i + n] + sums * scale_of(first_step)).astype(BF16)


def update_kernel(blocks, first_step, spread, send_row, total, *refs):
    arrived, (out, near_picked) = refs[:blocks], refs[blocks:]
    for i, n in steps(out.shape[1], 256):
        out[:, i : i + n] = updated_columns(first_step, spread, i, n, total, arrived)
    near_picked[...] = mm_nt(out[...], spread[0]).astype(BF16)


def last_kernel(blocks, first_step, spread, total, *refs):
    arrived, (out, held, sems) = refs[:blocks], refs[blocks:]
    copies = []
    for part, (i, n) in enumerate(steps(out.shape[1], LAST_COLUMNS)):
        held[:, i : i + n] = updated_columns(first_step, spread, i, n, total, arrived)
        at = pl.ds(i, n)
        copies.append(pltpu.make_async_copy(held.at[:, at], out.at[:, at], sems.at[part]))
        copies[-1].start()
    for copy in copies:
        copy.wait()


def shards(
    orbitals, rotation, cell_stiffness, cell_scale, potential, cell_nodes, send_rows, domain_rows
):
    domains = lax.axis_size("dom")
    bands = lax.axis_size("band")
    domain = lax.axis_index("dom")
    row_piece = orbitals[0]
    piece_rows, columns = row_piece.shape
    own_rows = domain_rows[0]
    width = columns // bands
    piece_shapes = (shape((width, piece_rows), BF16),) * bands
    pieces = list(call(
        rotate_kernel,
        piece_shapes,
        (row_piece.T, rotation),
        2 * piece_rows * columns * columns,
        scratch=[
            pltpu.VMEM((columns, piece_rows), BF16),
            pltpu.VMEM((columns, columns), BF16),
            pltpu.VMEM((bands, width, piece_rows), BF16),
            pltpu.SemaphoreType.DMA((2,)),
        ],
        in_specs=[ANY, ANY],
        vmem=ROTATE_VMEM,
    ))
    for k in reversed(range(1, bands)):
        pieces[k] = lax.ppermute(pieces[k], "band", [(i, i ^ k) for i in range(bands)])

    capacity = potential.shape[1]
    cells, nodes = cell_nodes.shape[1:]
    slots = send_rows.shape[2]
    nodes_pad = round_up(nodes, 256)
    slots_pad = round_up(slots, 16)
    far = far_groups(domains)
    blocks = 2 + len(far)
    ghosts = blocks * slots_pad
    even = domain % 2 == 0
    send_lists = [
        jnp.where(even, send_rows[0, 3], send_rows[0, 0]),
        jnp.where(even, send_rows[0, 0], send_rows[0, 3]),
    ] + [send_rows[0, g] for g in far]
    send_row = jnp.pad(
        jnp.stack(send_lists), ((0, 0), (0, slots_pad - slots)), constant_values=capacity
    )
    group = (cell_nodes[0] - capacity) // slots
    slot = (cell_nodes[0] - capacity) % slots
    block = jnp.where((group == 0) == even, 0, 1)
    for pos, g in enumerate(far):
        block = jnp.where(group == g, 2 + pos, block)
    ghost_index = capacity + block * slots_pad + slot
    node_list = jnp.where(cell_nodes[0] < capacity, cell_nodes[0], ghost_index)
    node_list = jnp.pad(
        node_list, ((0, 0), (0, nodes_pad - nodes)), constant_values=capacity + ghosts
    ).reshape(-1)
    node_row = node_list[None, :]
    stiffness = jnp.pad(cell_stiffness, ((0, nodes_pad - nodes), (0, nodes_pad - nodes)))

    cell_total = (own_rows - FACE_NODES) // (DEGREE * FACE_NODES)
    cell_live = jnp.arange(cell_scale.shape[1], dtype=jnp.int32) < cell_total
    weight = jnp.where(cell_live, cell_scale[0], jnp.zeros_like(cell_scale[0]))
    weight = jnp.repeat(weight, nodes_pad)[None, :]

    local_rows = cells * nodes_pad
    cell_flops = 2 * local_rows * nodes_pad
    to_ghost, to_own, scatter, spread, far_near, pairing = call(
        functools.partial(couple_kernel, capacity),
        (
            shape((blocks, ghosts, slots_pad), BF16),
            shape((ghosts, capacity), BF16),
            shape((local_rows, capacity), BF16),
            shape((blocks, slots_pad, capacity), BF16),
            shape((slots_pad, slots_pad), BF16),
            shape((3 * slots_pad, 2 * slots_pad), BF16),
        ),
        (weight, node_row, send_row, stiffness),
        (cell_flops + 2 * local_rows * (ghosts + capacity)) * ghosts,
        scratch=[pltpu.VMEM((ghosts, local_rows), BF16)],
    )
    block_shape = shape((width, slots_pad), BF16)
    keep = (jnp.arange(capacity, dtype=jnp.int32) < own_rows).astype(jnp.int32)[None, :]
    near_rows = width if far else round_up(width, 16) + DIGIT_ROWS
    digits = jnp.pad(
        jnp.stack([send_row[0] // DIGIT, send_row[0] % DIGIT]), ((0, DIGIT_ROWS - 2), (0, 0))
    ).astype(BF16)
    current, near_picked = call(
        join_kernel,
        (shape((width, capacity), BF16), shape((near_rows, slots_pad), BF16)),
        (send_row, keep, digits, to_ghost, *pieces),
        2 * slots_pad * capacity * width,
        scratch=[pltpu.VMEM((bands, width, piece_rows), BF16)],
        in_specs=[VMEM, VMEM, VMEM, ANY] + [VMEM] * bands,
    )
    previous = None
    parcel_rows = round_up(width, 16) + coupling_rows(slots_pad)
    terms_shape = shape((blocks, width, slots_pad), F32)
    terms_flops = 4 * ghosts * capacity * width
    for filter_step in range(FILTER_STEPS):
        first, last = filter_step == 0, filter_step == FILTER_STEPS - 1
        if first or far:
            near = swap(near_picked, 0)
            terms, *picked = call(
                terms_kernel,
                (terms_shape,) + (block_shape,) * (blocks - 1),
                (spread, to_own, current),
                terms_flops,
            )
        if far:
            arrived = [near, *exchange(picked, False)]
            ready = terms
        else:
            if first:
                same = call(
                    functools.partial(same_kernel, capacity),
                    shape((slots_pad, slots_pad), BF16),
                    (near,),
                    slots_pad * slots_pad,
                )
                ready = call(
                    parcel_kernel,
                    shape((parcel_rows, 2 * slots_pad), BF16),
                    (terms, to_ghost, near, picked[0]),
                    2 * slots_pad * slots_pad * width,
                )
            parcel = swap(ready, 1)
            first_parcel = parcel if first else first_parcel
        history = () if first else (previous,)
        near_wanted = not far and not last
        wanted = (terms,) if near_wanted else ()
        head, *near_head = call(
            functools.partial(cells_kernel, first, near_wanted),
            (shape((width, capacity), F32),) + (shape((width, 2 * slots_pad), F32),) * near_wanted,
            (weight, node_row, stiffness, scatter, spread, potential, current, ready, *history, *wanted),
            (cell_flops + 4 * local_rows * capacity) * width,
            scratch=[pltpu.VMEM((width, local_rows), BF16)] + [pltpu.VMEM((width, nodes_pad), BF16)] * cells,
            in_specs=[VMEM] * 7 + [ANY] + [VMEM] * len((*history, *wanted)),
        )
        own_flops = 2 * capacity * ghosts * width
        if far:
            sums = call(
                ghost_kernel,
                (block_shape,) * blocks,
                (terms, to_ghost, *arrived),
                2 * ghosts * ghosts * width,
            )
            returned = [swap(sums[0], 0), *exchange(sums[1:], True)]
            total = call(
                functools.partial(own_kernel, first),
                shape((width, capacity), F32),
                (to_own, head, *arrived),
                own_flops,
            )
        else:
            if last:
                sent = call(
                    near_kernel,
                    block_shape,
                    (terms, to_ghost, near, parcel, head),
                    2 * ghosts * slots_pad * width,
                    in_specs=[VMEM] * 4 + [ANY],
                )
            else:
                sent_shape = shape((width, 2 * slots_pad), BF16)
                coupled_shape = shape((slots_pad, 2 * slots_pad), BF16)
                sent, *coupled_out = call(
                    functools.partial(pair_kernel, first),
                    (sent_shape, coupled_shape) if first else (sent_shape,),
                    (near, picked[0], parcel, *near_head, pairing)
                    + ((first_parcel, far_near) if first else (coupled,)),
                    8 * ghosts * slots_pad * width,
                )
                coupled = coupled_out[0] if first else coupled
            returned = [swap(sent, 0)]
            total = call(
                functools.partial(paired_own_kernel, first),
                shape((width, capacity), F32),
                (to_own, head, spread, near, picked[0], parcel, first_parcel),
                own_flops,
            )
        update_flops = 2 * capacity * (ghosts + slots_pad * len(returned)) * width
        if last:
            current = call(
                functools.partial(last_kernel, len(returned), first),
                shape((width, capacity), BF16),
                (spread, total, *returned),
                update_flops,
                scratch=[
                    pltpu.VMEM((width, capacity), BF16),
                    pltpu.SemaphoreType.DMA((len(steps(capacity, LAST_COLUMNS)),)),
                ],
                out_specs=ANY,
            )
        elif not far:
            following, near, far_picked, terms, ready = call(
                functools.partial(advance_kernel, first),
                (
                    shape((width, capacity), BF16),
                    block_shape,
                    block_shape,
                    terms_shape,
                    shape((width, 2 * slots_pad), BF16),
                ),
                (spread, same, to_own, to_ghost, total, sent, *returned),
                update_flops + terms_flops,
            )
            picked = [far_picked]
            previous, current = current, following
        else:
            following, near_picked = call(
                functools.partial(update_kernel, len(returned), first),
                (shape((width, capacity), BF16), block_shape),
                (spread, send_row, total, *returned),
                update_flops,
            )
            previous, current = current, following
    return current.T[None]


def solution(mesh):
    return jax.shard_map(
        shards,
        mesh=mesh,
        in_specs=(
            P("dom", "band", None),
            P(),
            P(),
            P("dom", None),
            P("dom", None),
            P("dom", None, None),
            P("dom", None, None),
            P("dom"),
        ),
        out_specs=P("dom", None, "band"),
        check_vma=False,
    )
```
